32 devices in a mesh: groups: 2 (over y), rows: 4 (over z), cols: 2 (over x), maps: 2 (over core).
Axes of the slice: x: 2, y: 2, z: 4, core: 2. Of those that a mesh axis runs over, the one named last changes fastest.
Arguments:
- drivers: bfloat16 [4, 16, 512, 256], P(('groups', 'maps'), None, 'rows', 'cols'), parts along dimension 0, may hold values from -6 to 6
- observed: bfloat16 [4, 512, 256], P(('groups', 'maps'), 'rows', 'cols'), parts along dimension 0, may hold values from 0.099609375 to 3
- confidence: bfloat16 [4, 512, 256], P(('groups', 'maps'), 'rows', 'cols'), parts along dimension 0, may hold values from 0.19921875 to 2
- land_mask: int32 [1024, 256], P(('groups', 'rows'), 'cols'), parts along dimension 0, may hold values from 0 to 1, as said below
- ownership: int32 [1024, 4], P(('groups', 'rows'), 'cols'), parts along dimension 0, may hold values from -1 to 7, as said below
- first_layer: bfloat16 [16, 128], replicated, may hold values from -1.5 to 1.5
- second_layer: bfloat16 [128, 128], replicated, may hold values from -0.5 to 0.5
- output_layer: bfloat16 [128], replicated, may hold values from -0.5 to 0.5
Outputs:
- first_gradient: float32 [32, 128], P('groups'), parts along dimension 0
- second_gradient: float32 [256, 128], P('groups'), parts along dimension 0
- output_gradient: float32 [256], P('groups'), parts along dimension 0
- source_scaling: float32 [4, 512, 256], P(('groups', 'maps'), 'rows', 'cols'), parts along dimension 0
- target_scaling: float32 [4, 512, 256], P(('groups', 'maps'), 'rows', 'cols'), parts along dimension 0
The draws below stay inside these ranges and needn't reach their ends.
There are 2 independent parts, one for each index of `groups`. The reference program is written for one: setup_inputs(seed, part) draws one part's arguments, and reference() takes and returns one part's arrays. A program takes and returns all parts, laid end to end along the dimension named above; an argument that names none is the same for every part. Nothing has to cross between parts.
Inputs may be any that keep to these rules, and one draw needn't show every extreme that they name: `ownership`: -1 marks a block without land. Every device of rows and cols owns exactly 96 land blocks of the slab, and at most 32 blocks of one device's tile; some tile gives 32 blocks to one owner. `land_mask`: land cells lie only in blocks whose ownership is not -1, and every such block holds one or more.
All inputs are finite; a program needn't handle non-finite values.
Results may differ from the reference program's by a relative error of at most 0.0013.
Values may be sent and summed in bfloat16 or wider, within the bound.
No kernel may reach another device: no remote copies, remote signals or barrier semaphores. Data moves between devices by JAX's collectives and lax.ppermute only.
A program may use at most 64 MiB of HBM per device.

```python
import math
import jax
import jax.numpy as jnp
from jax import lax

FEAT = 16
HID = 128
TR = 128
TC = 128
BLK = 64
RADIUS = 24
ITERS = 2
MAPS = 2
NY = 512
NX = 256
OWNERS = 8
NB = 256
CAP = 32
LAND = 768


def land_layout(key):
    base = jax.random.fold_in(key, 1234)
    key_bias, key_noise, key_order, key_favored, key_cells, key_forced = jax.random.split(base, 6)
    tile_bias = jax.random.randint(key_bias, (OWNERS,), 0, 4)
    favored = jax.random.randint(key_favored, (), 0, OWNERS)
    tile_bias = jnp.where(jnp.arange(OWNERS) == favored, 5, tile_bias)
    noise = jax.random.randint(key_noise, (OWNERS, NB), 0, 3)
    tiebreak = jax.random.permutation(key_order, OWNERS * NB).reshape(OWNERS, NB)
    ranking = (tile_bias[:, None] * 3 + noise) * (OWNERS * NB) + tiebreak
    order = jnp.argsort(-ranking.reshape(-1), stable=True)
    landed = jnp.zeros((OWNERS * NB,), jnp.int32).at[order[:LAND]].set(1)
    counter = jnp.cumsum(landed) - 1
    owner_flat = jnp.where(landed > 0, counter // CAP % OWNERS, -1).astype(jnp.int32)
    cells = jax.random.randint(key_cells, (OWNERS * NB, BLK), 0, 4) > 0
    forced = jax.random.randint(key_forced, (OWNERS * NB, 1), 0, BLK)
    cells = cells | (jnp.arange(BLK)[None, :] == forced)
    mask_flat = jnp.where((landed[:, None] > 0) & cells, 1, 0).astype(jnp.int32)
    return (owner_flat, mask_flat)


def draw_ownership(key, part):
    owner_flat, mask_flat = land_layout(key)
    grid = owner_flat.reshape(NY // TR, NX // TC, TR, TC // BLK)
    return grid.transpose(0, 2, 1, 3).reshape(NY, NX // BLK)


def draw_land_mask(key, part):
    owner_flat, mask_flat = land_layout(key)
    grid = mask_flat.reshape(NY // TR, NX // TC, TR, TC // BLK, BLK)
    return grid.transpose(0, 2, 1, 3, 4).reshape(NY, NX)


def steps_of(stream_key, shape, cuts, least, top_value):
    factor_of, own = 1.0, jax.random.fold_in(stream_key, 6)
    for axis_at, shards_of in cuts:
        heights = jnp.exp(jax.random.uniform(jax.random.fold_in(own, axis_at), (shards_of,), jnp.float32, least / len(cuts), top_value / len(cuts)))
        factor_of = factor_of * jnp.repeat(heights, shape[axis_at] // shards_of).reshape([-1 if axis == axis_at else 1 for axis in range(len(shape))])
    return factor_of


def bell_draw(stream_key, dims, spread, most, pieces=(), dtype=jnp.bfloat16):
    result = spread * jax.random.normal(stream_key, dims, jnp.float32)
    if pieces:
        result = result * steps_of(stream_key, dims, pieces, -0.22, 0.18)
    return jnp.clip(result, -most, most).astype(dtype)


def setup_inputs(seed: int = 0, part: int = 0) -> dict:
    key_of = jax.random.split(jax.random.key(seed), 9)
    own_keys = jax.random.split(jax.random.fold_in(key_of[8], part), 9)
    return {
        "drivers": bell_draw(own_keys[0], (MAPS, FEAT, NY, NX), 1.0, 6.0, ((0, 2), (2, 4), (3, 2))),
        "observed": jnp.clip(jnp.exp(math.log(3.0) - 3.4051113 * jax.random.uniform(own_keys[1], (MAPS, NY, NX), jnp.float32) ** steps_of(own_keys[1], (MAPS, NY, NX), ((0, 2), (1, 4), (2, 2)), -0.2, 0.2)), 0.099609375, 3.0).astype(jnp.bfloat16),
        "confidence": jnp.clip(jnp.exp(math.log(2.0) - 2.306499 * jax.random.uniform(own_keys[2], (MAPS, NY, NX), jnp.float32) ** steps_of(own_keys[2], (MAPS, NY, NX), ((0, 2), (1, 4), (2, 2)), -0.2, 0.2)), 0.19921875, 2.0).astype(jnp.bfloat16),
        "land_mask": draw_land_mask(jax.random.fold_in(jax.random.fold_in(key_of[8], part), 71), part),
        "ownership": draw_ownership(jax.random.fold_in(jax.random.fold_in(key_of[8], part), 71), part),
        "first_layer": bell_draw(key_of[5], (FEAT, HID), FEAT ** -0.5, 1.5),
        "second_layer": bell_draw(key_of[6], (HID, HID), HID ** -0.5, 0.5),
        "output_layer": bell_draw(key_of[7], (HID,), HID ** -0.5, 0.5),
    }


HIGHEST = lax.Precision.HIGHEST
BACKGROUND = 0.1


def silu_slope(value):
    logistic = jax.nn.sigmoid(value)
    return logistic * (1.0 + value * (1.0 - logistic))


def imitate(inputs, targets, first_layer, second_layer, output_layer):
    pre_first = jnp.einsum("nmfb,fh->nmbh", inputs.astype(jnp.float32), first_layer.astype(jnp.float32))
    hidden_first = jax.nn.silu(pre_first).astype(jnp.bfloat16)
    pre_second = jnp.einsum("nmbh,hk->nmbk", hidden_first.astype(jnp.float32), second_layer.astype(jnp.float32))
    hidden_second = jax.nn.silu(pre_second).astype(jnp.bfloat16)
    score = jnp.einsum("nmbk,k->nmb", hidden_second.astype(jnp.float32), output_layer.astype(jnp.float32))
    imitated = jax.nn.softplus(score)
    observed_part = targets[:, :, 0].astype(jnp.float32)
    weighted_part = targets[:, :, 1].astype(jnp.float32)
    delta_score = weighted_part * (imitated - observed_part) * jax.nn.sigmoid(score)
    output_grad = jnp.einsum("nmb,nmbk->k", delta_score, hidden_second.astype(jnp.float32))
    delta_second = (delta_score[..., None] * output_layer.astype(jnp.float32) * silu_slope(pre_second)).astype(jnp.bfloat16)
    second_grad = jnp.einsum("nmbh,nmbk->hk", hidden_first.astype(jnp.float32), delta_second.astype(jnp.float32))
    back_first = jnp.einsum("nmbk,hk->nmbh", delta_second.astype(jnp.float32), second_layer.astype(jnp.float32))
    delta_first = (back_first * silu_slope(pre_first)).astype(jnp.bfloat16)
    first_grad = jnp.einsum("nmfb,nmbh->fh", inputs.astype(jnp.float32), delta_first.astype(jnp.float32))
    return imitated, (first_grad, second_grad, output_grad)


def smooth(field):
    offsets = jnp.arange(-RADIUS, RADIUS + 1).astype(jnp.float32)
    weights = jnp.exp(-4.5 * offsets * offsets / (RADIUS * RADIUS))
    weights = weights / jnp.sum(weights)
    stacked = field[:, None]
    kernel_rows = weights.reshape(1, 1, -1, 1)
    kernel_cols = weights.reshape(1, 1, 1, -1)
    along = lax.conv_general_dilated(stacked, kernel_rows, (1, 1), ((RADIUS, RADIUS), (0, 0)), precision=HIGHEST)
    along = lax.conv_general_dilated(along, kernel_cols, (1, 1), ((0, 0), (RADIUS, RADIUS)), precision=HIGHEST)
    return along[:, 0]


def reference(drivers, observed, confidence, land_mask, ownership, first_layer, second_layer, output_layer):
    mask_float = land_mask.astype(jnp.float32)
    weighted = (confidence.astype(jnp.float32) * mask_float[None]).astype(jnp.bfloat16)
    per_row = NX // BLK
    total_blocks = NY * per_row
    blocks = drivers.reshape(MAPS, FEAT, NY, per_row, BLK).transpose(2, 3, 0, 1, 4).reshape(total_blocks, MAPS, FEAT, BLK)
    paired = jnp.stack([observed, weighted], axis=1)
    targets = paired.reshape(MAPS, 2, NY, per_row, BLK).transpose(2, 3, 0, 1, 4).reshape(total_blocks, MAPS, 2, BLK)
    land_index = jnp.nonzero(ownership.reshape(total_blocks) >= 0, size=LAND)[0].astype(jnp.int32)
    group_size = math.gcd(LAND, 512)
    grouped = land_index.reshape(LAND // group_size, group_size)

    def visit(totals, indices):
        imitated, grads = imitate(jnp.take(blocks, indices, axis=0), jnp.take(targets, indices, axis=0), first_layer, second_layer, output_layer)
        return (totals[0] + grads[0], totals[1] + grads[1], totals[2] + grads[2]), imitated

    start = (jnp.zeros((FEAT, HID), jnp.float32), jnp.zeros((HID, HID), jnp.float32), jnp.zeros((HID,), jnp.float32))
    totals, imitated = lax.scan(visit, start, grouped)
    imitated_blocks = jnp.zeros((total_blocks, MAPS, BLK), jnp.float32).at[land_index].set(imitated.reshape(LAND, MAPS, BLK))
    imitated_map = imitated_blocks.reshape(NY, per_row, MAPS, BLK).transpose(2, 0, 1, 3).reshape(MAPS, NY, NX)
    weight_total = jnp.sum(weighted.astype(jnp.float32))
    source = mask_float[None] * imitated_map + BACKGROUND
    target = mask_float[None] * observed.astype(jnp.float32) + BACKGROUND
    source = source / (jnp.sum(source, axis=(1, 2)) / (NY * NX))[:, None, None]
    target = target / (jnp.sum(target, axis=(1, 2)) / (NY * NX))[:, None, None]
    target_scaling = jnp.ones_like(source)
    source_scaling = source
    for step in range(ITERS):
        source_scaling = source / smooth(target_scaling)
        target_scaling = target / smooth(source_scaling)
    return (totals[0] / weight_total, totals[1] / weight_total, totals[2] / weight_total, source_scaling, target_scaling)
```

```python
import functools

import jax
import jax.numpy as jnp
import ml_dtypes
import numpy as np
from jax import lax
from jax.experimental import pallas as pl
from jax.experimental.pallas import tpu as pltpu
from jax.sharding import PartitionSpec as P

RADIUS = 24
F32 = jnp.float32
BF = jnp.bfloat16


def net_kernel(drv, obs, conf, mask, w1, w2, wo, g_out, src_out, tgt_out, left_out, right_out):
    rows = mask.shape[0]
    hid = w2.shape[0]
    feat = w1.shape[0]
    w1h = (w1[...].astype(F32) * 0.5).T.astype(BF)
    w2f = w2[...].astype(F32)
    w2h = (w2f * 0.5).T.astype(BF)
    w2b = w2[...]
    wo_row = wo[...].astype(F32)
    wo_col = jnp.broadcast_to(wo_row * 0.5, (128, hid)).T
    wo8 = jnp.broadcast_to(wo_row, (8, hid)).astype(BF)
    sub = lax.broadcasted_iota(jnp.int32, (8, 128), 0)

    def body(i, carry):
        second, first, outg, wsum, ssum, tsum = carry
        r0 = pl.multiple_of(i * 16, 16)
        x3 = jnp.swapaxes(drv[0, :, pl.ds(r0, 16), :].astype(F32), 0, 1).astype(BF)
        ob = obs[0, pl.ds(r0, 16), :].astype(F32)
        cf = conf[0, pl.ds(r0, 16), :].astype(F32)
        mk = mask[pl.ds(r0, 16), :].astype(F32)
        wm = (cf * mk).astype(BF).astype(F32)
        tg = ob * mk + 0.1
        tgt_out[pl.ds(r0, 16), :] = tg
        wsum += wm[:8] + wm[8:]
        tsum += tg[:8] + tg[8:]
        for half in range(2):
            x = jnp.concatenate([x3[half * 8 + r] for r in range(8)], axis=1)
            p1 = jnp.dot(w1h, x, preferred_element_type=F32)
            t1 = jnp.tanh(p1)
            u1 = 1.0 + t1
            h1 = (p1 * u1).astype(BF)
            s1 = u1 * (0.5 + (0.5 * p1) * (1.0 - t1))
            p2 = jnp.dot(w2h, h1, preferred_element_type=F32)
            t2 = jnp.tanh(p2)
            u2 = 1.0 + t2
            h2 = (p2 * u2).astype(BF)
            sc8 = jnp.dot(wo8, h2, preferred_element_type=F32)
            score = sc8[:, 0:128]
            for r in range(1, 8):
                score = jnp.where(sub == r, sc8[:, r * 128:(r + 1) * 128], score)
            e = jnp.exp(-jnp.abs(score))
            imitated = jnp.maximum(score, 0.0) + jnp.log1p(e)
            sig = jnp.where(score >= 0, 1.0, e) / (1.0 + e)
            sl = slice(half * 8, half * 8 + 8)
            delta = wm[sl] * (imitated - ob[sl]) * sig
            sr = mk[sl] * imitated + 0.1
            src_out[pl.ds(r0 + half * 8, 8), :] = sr
            ssum += sr
            drow = jnp.concatenate([jnp.broadcast_to(delta[r:r + 1], (8, 128)) for r in range(8)], axis=1)
            dhi = drow.astype(BF)
            dlo = (drow - dhi.astype(F32)).astype(BF)
            sub1 = lax.broadcasted_iota(jnp.int32, (8, 1024), 0)
            dmix = jnp.where(sub1 == 0, dhi.astype(F32), dlo.astype(F32)).astype(BF)
            dw = jnp.concatenate([
                wo_col * jnp.concatenate([drow[:, r * 128:(r + 1) * 128]] * 16, axis=0) for r in range(8)], axis=1)
            d2 = (dw * (u2 * (1.0 + p2 * (1.0 - t2)))).astype(BF)
            nt = (((1,), (1,)), ((), ()))
            second += lax.dot_general(h1, d2, nt, preferred_element_type=F32)
            outg += lax.dot_general(dmix, h2, nt, preferred_element_type=F32)
            back = jnp.dot(w2b, d2, preferred_element_type=F32)
            d1 = (back * s1).astype(BF)
            first += lax.dot_general(x, d1, nt, preferred_element_type=F32)
        return second, first, outg, wsum, ssum, tsum

    z8 = jnp.zeros((8, 128), F32)
    second, first, outg, wsum, ssum, tsum = lax.fori_loop(
        0, rows // 16, body,
        (jnp.zeros((hid, hid), F32), jnp.zeros((feat, hid), F32), z8, z8, z8, z8))
    g_out[0:hid, :] = second
    g_out[hid:hid + feat, :] = first
    og = outg[0:1] + outg[1:2]
    lane = lax.broadcasted_iota(jnp.int32, (8, 128), 1)
    me = lax.axis_index("maps")
    tot = lambda v: jnp.sum(jnp.sum(v, axis=1, keepdims=True), axis=0, keepdims=True)
    extra = jnp.where(sub == 0, og, 0.0)
    extra = jnp.where(sub == 1, tot(wsum), extra)
    extra = jnp.where(sub == 2 + me, tot(ssum), extra)
    extra = jnp.where(sub == 4 + me, tot(tsum), extra)
    g_out[hid + feat:hid + feat + 8, :] = extra
    lanes = lax.broadcasted_iota(jnp.int32, (rows, 128), 1)
    left, right = edge_strips(src_out[...], tgt_out[...], lanes)
    left_out[...] = left
    if lax.axis_size("cols") == 2:
        right = jnp.where(lax.axis_index("cols") == 0, right, left)
    right_out[...] = right

def net(drivers, observed, confidence, land_mask, w1, w2, wo):
    feat, hid = w1.shape
    R, C = land_mask.shape
    return pl.pallas_call(
        net_kernel,
        out_shape=(jax.ShapeDtypeStruct((hid + feat + 8, 128), F32),
                   *[jax.ShapeDtypeStruct((R, C), F32)] * 4),
        name="net",
    )(drivers, observed, confidence, land_mask, w1, w2, wo.reshape(1, hid))


def edge_strips(src, tgt, lane):
    right = jnp.where(lane >= 128 - 3 * RADIUS, src, pltpu.roll(tgt, 2 * RADIUS, 1))
    left = jnp.where(lane < 3 * RADIUS, src, pltpu.roll(tgt, 128 - 2 * RADIUS, 1))
    return left, right


def left_block(strip, lane):
    src = jnp.where(lane >= 128 - 3 * RADIUS, strip, 0.0)
    tgt = jnp.where(lane >= 128 - 2 * RADIUS, pltpu.roll(strip, 128 - 2 * RADIUS, 1), 0.0)
    return src, tgt


def right_block(strip, lane):
    src = jnp.where(lane < 3 * RADIUS, strip, 0.0)
    tgt = jnp.where(lane < 2 * RADIUS, pltpu.roll(strip, 2 * RADIUS, 1), 0.0)
    return src, tgt


def widen(src, tgt, strips):
    lane = lax.broadcasted_iota(jnp.int32, src.shape, 1)
    if not strips:
        return src, tgt
    if len(strips) == 1:
        at_left = lax.axis_index("cols") == 0
        rs, rt = right_block(strips[0], lane)
        ls, lt = left_block(strips[0], lane)
        wide_src = jnp.concatenate([jnp.where(at_left, src, ls), jnp.where(at_left, rs, src)], axis=1)
        wide_tgt = jnp.concatenate([jnp.where(at_left, tgt, lt), jnp.where(at_left, rt, tgt)], axis=1)
        return wide_src, wide_tgt
    ls, lt = left_block(strips[0], lane)
    rs, rt = right_block(strips[1], lane)
    return jnp.concatenate([ls, src, rs], axis=1), jnp.concatenate([lt, tgt, rt], axis=1)


def halo_kernel(src_ref, tgt_ref, *refs):
    strips = [ref[...] for ref in refs[:-2]]
    up_ref, down_ref = refs[-2:]
    src, tgt = widen(src_ref[...], tgt_ref[...], strips)
    far, near = 3 * RADIUS, 2 * RADIUS
    rows = src.shape[0]
    up_ref[0:far, :] = src[0:far]
    up_ref[far:far + near, :] = tgt[0:near]
    down_ref[0:far, :] = src[rows - far:rows]
    down_ref[far:far + near, :] = tgt[rows - near:rows]


def halo(src, tgt, strips):
    width = src.shape[1] * (1 + len(strips))
    shape = jax.ShapeDtypeStruct((5 * RADIUS, width), F32)
    return pl.pallas_call(halo_kernel, out_shape=(shape, shape), name="halo")(src, tgt, *strips)


def parts(value):
    high = value.astype(BF)
    return high, (value - high.astype(F32)).astype(BF)


def product(left, right):
    (lh, ll), (rh, rl) = left, right
    dot = functools.partial(jnp.dot, preferred_element_type=F32)
    return dot(lh, rh) + (dot(lh, rl) + dot(ll, rh))


def sinkhorn_kernel(first_last, src_ref, tgt_ref, above_ref, below_ref, brow_ref, bcol_ref, krow_ref, kcol_ref, *refs):
    strips = [ref[...] for ref in refs[:-2]]
    source_out, target_out = refs[-2:]
    far, near = 3 * RADIUS, 2 * RADIUS
    rows = src_ref.shape[0]
    wide = above_ref.shape[1]
    src, tgt = widen(src_ref[...], tgt_ref[...], strips)
    source = jnp.concatenate([above_ref[0:far, :], src, below_ref[0:far, :]], axis=0)
    target = jnp.concatenate([above_ref[far:far + near, :], tgt, below_ref[far:far + near, :]], axis=0)
    rows_at, cols_at = lax.axis_index("rows"), lax.axis_index("cols")
    row_first = (rows_at == 0).astype(F32)
    row_last = (rows_at == lax.axis_size("rows") - 1).astype(F32)
    krow = 1.0 - row_first * krow_ref[0] - row_last * krow_ref[1]
    if len(strips) == 2:
        col_first = (cols_at == 0).astype(F32)
        col_last = (cols_at == lax.axis_size("cols") - 1).astype(F32)
        kcol = 1.0 - col_first * kcol_ref[0:1, :] - col_last * kcol_ref[1:2, :]
        own = 128
    else:
        kcol = 1.0 - kcol_ref[0:1, :] - kcol_ref[1:2, :]
        own = pl.multiple_of(cols_at * 128, 128) if strips else 0
    krow = jnp.concatenate([krow] * (wide // 128), axis=1)
    brow = (brow_ref[0], brow_ref[1])
    bcol = (bcol_ref[0], bcol_ref[1])

    def smooth(field, count, columns):
        bands = tuple(band[0:count, 0:count + near] for band in brow)
        return product(parts(product(bands, parts(field))), columns)

    def ratio(top, bottom):
        inside = top > 0.0
        return jnp.where(inside, top / jnp.where(inside, bottom, 1.0), 0.0)

    scaling = source / (krow * kcol)
    scaling = ratio(target, smooth(scaling, rows + 2 * near, bcol))
    scaling = ratio(source[near:near + rows + near], smooth(scaling, rows + near, bcol))
    bottom = smooth(scaling, rows, tuple(bcol_ref[i, :, pl.ds(own, 128)] for i in range(2)))
    if len(strips) == 1:
        source_out[...] = jnp.where(cols_at == 0, scaling[RADIUS:RADIUS + rows, 0:128], scaling[RADIUS:RADIUS + rows, 128:256])
    else:
        source_out[...] = scaling[RADIUS:RADIUS + rows, own:own + 128]
    target_out[...] = tgt_ref[...] / bottom


def split_table(table):
    high = table.astype(ml_dtypes.bfloat16)
    low = (table - high.astype(np.float64)).astype(ml_dtypes.bfloat16)
    return np.stack([high, low])


def taps():
    offsets = np.arange(-RADIUS, RADIUS + 1, dtype=np.float64)
    weights = np.exp(-4.5 * offsets * offsets / (RADIUS * RADIUS))
    return weights / weights.sum()


def tails(start, count, end):
    weights = taps()
    before, after = np.zeros(count), np.zeros(count)
    for at in range(count):
        if at >= start:
            before[at] = weights[: max(0, RADIUS - (at - start))].sum()
        if at < end:
            after[at] = weights[: max(0, RADIUS - (end - 1 - at))].sum()
    return np.stack([before, after])


def sinkhorn(src, tgt, above, below, strips):
    rows, cols = src.shape
    wide = above.shape[1]
    weights = taps()

    def toeplitz(count_out, count_in, shift):
        offset = np.arange(count_in)[None, :] - np.arange(count_out)[:, None] + shift
        inside = (offset >= 0) & (offset <= 2 * RADIUS)
        return np.where(inside, weights[np.clip(offset, 0, 2 * RADIUS)], 0.0)

    brow = split_table(toeplitz(rows + 4 * RADIUS, rows + 6 * RADIUS, 0))
    bcol = split_table(toeplitz(wide, wide, RADIUS))
    krow = tails(3 * RADIUS, rows + 6 * RADIUS, 3 * RADIUS + rows)
    krow = np.broadcast_to(krow[:, :, None], krow.shape + (128,)).astype(np.float32)
    if len(strips) == 2:
        kcol = tails(cols, wide, 2 * cols)
    else:
        kcol = tails(0, wide, wide)
    kcol = np.concatenate([kcol, np.zeros((6, wide))]).astype(np.float32)
    shape = jax.ShapeDtypeStruct((rows, cols), F32)
    return pl.pallas_call(functools.partial(sinkhorn_kernel, None), out_shape=(shape, shape), name="sinkhorn")(
        src, tgt, above, below, jnp.asarray(brow), jnp.asarray(bcol), jnp.asarray(krow), jnp.asarray(kcol), *strips
    )


def finish_kernel(cells, hid, feat, *refs):
    count = len(refs) - 7
    sums = refs[0][...]
    for ref in refs[1:count]:
        sums = sums + ref[...]
    source_ref, target_ref = refs[count:count + 2]
    first_out, second_out, output_out, source_out, target_out = refs[count + 2:]
    tail = sums[hid + feat:hid + feat + 8]
    me = lax.axis_index("maps")
    maps = lax.axis_size("maps")
    inverse = 1.0 / tail[1:2]
    second_out[...] = sums[0:hid] * inverse
    first_out[...] = sums[hid:hid + feat] * inverse
    output_out[...] = tail[0:1] * inverse
    source_mean, target_mean = tail[2:3], tail[2 + maps:3 + maps]
    for other in range(1, maps):
        source_mean = jnp.where(me == other, tail[2 + other:3 + other], source_mean)
        target_mean = jnp.where(me == other, tail[2 + maps + other:3 + maps + other], target_mean)
    source_mean, target_mean = source_mean * (1.0 / cells), target_mean * (1.0 / cells)
    ratio = source_mean / target_mean
    source_out[0] = source_ref[...] * (1.0 / (source_mean * ratio))
    target_out[0] = target_ref[...] * (ratio * ratio)


def finish(sums, source, target, cells, hid, feat):
    shape = jax.ShapeDtypeStruct((1,) + source.shape, F32)
    return pl.pallas_call(
        functools.partial(finish_kernel, cells, hid, feat),
        out_shape=(
            jax.ShapeDtypeStruct((feat, hid), F32),
            jax.ShapeDtypeStruct((hid, hid), F32),
            jax.ShapeDtypeStruct((1, hid), F32),
            shape,
            shape,
        ),
        name="finish",
    )(*sums, source, target)


def swap(value, axis, step):
    return lax.ppermute(value, axis, [(i, i ^ step) for i in range(lax.axis_size(axis))])


def local(
    drivers, observed, confidence, land_mask, ownership, first_layer, second_layer, output_layer
):
    feat, hid = first_layer.shape
    row_count, col_count = lax.axis_size("rows"), lax.axis_size("cols")
    cells = land_mask.size * row_count * col_count
    sums, src, tgt, left, right = net(
        drivers, observed, confidence, land_mask, first_layer, second_layer, output_layer
    )
    if col_count == 1:
        strips = []
    elif col_count == 2:
        strips = [swap(right, "cols", 1)]
    else:
        strips = [
            lax.ppermute(right, "cols", [(i, i + 1) for i in range(col_count - 1)]),
            lax.ppermute(left, "cols", [(i + 1, i) for i in range(col_count - 1)]),
        ]
    up, down = halo(src, tgt, strips)
    above = lax.ppermute(down, "rows", [(i, i + 1) for i in range(row_count - 1)])
    below = lax.ppermute(up, "rows", [(i + 1, i) for i in range(row_count - 1)])
    source, target = sinkhorn(src, tgt, above, below, strips)
    steps = []
    for axis in ("maps", "cols", "rows"):
        step = 1
        while step < lax.axis_size(axis):
            steps.append((axis, step))
            step *= 2
    pending = [sums]
    for axis, step in steps:
        total = pending[0] if len(pending) == 1 else pending[0] + pending[1]
        pending = [total, swap(total, axis, step)]
    first, second, output, source, target = finish(pending, source, target, cells, hid, feat)
    return first, second, output.reshape(hid), source, target


def solution(mesh):
    in_specs = (
        P(("groups", "maps"), None, "rows", "cols"),
        P(("groups", "maps"), "rows", "cols"),
        P(("groups", "maps"), "rows", "cols"),
        P(("groups", "rows"), "cols"),
        P(("groups", "rows"), "cols"),
        P(),
        P(),
        P(),
    )
    out_specs = (
        P("groups", None),
        P("groups", None),
        P("groups"),
        P(("groups", "maps"), "rows", "cols"),
        P(("groups", "maps"), "rows", "cols"),
    )
    return jax.shard_map(local, mesh=mesh, in_specs=in_specs, out_specs=out_specs, check_vma=False)
```

```python
import functools

import jax
import jax.numpy as jnp
import ml_dtypes
import numpy as np
from jax import lax
from jax.experimental import pallas as pl
from jax.experimental.pallas import tpu as pltpu
from jax.sharding import PartitionSpec as P

RADIUS = 24
BACKGROUND = 0.1
UNIT = 8
F32 = jnp.float32
BF = jnp.bfloat16
NT = (((1,), (1,)), ((), ()))


def net_kernel(sides, *refs):
    inputs, refs = refs[0:7], refs[7:]
    keep_out, send_out, src_out, tgt_out = refs[0:4]
    strip_outs, scr = refs[4:4 + sides], refs[4 + sides:]
    held, arrived, scr = scr[-8:-1], scr[-1], scr[:-8]
    copies = [pltpu.make_async_copy(a, b, arrived.at[k]) for k, (a, b) in enumerate(zip(inputs, held))]
    for copy in copies:
        copy.start()
    drv, obs, conf, mask, w1, w2, wo = held
    for copy in copies:
        copy.wait()
    rows = mask.shape[0]
    hid = w2.shape[0]
    feat = w1.shape[0]
    units = rows // UNIT
    wide = UNIT * 128
    TILE = 256
    h1s, s1s, p2s, d2s = scr[0:3], scr[3:6], scr[6:9], scr[9:12]
    xs, obf, wmf, mkf, acc_second, acc_first, acc_outg, wide_wo = scr[12:]
    w1h = (w1[...].astype(F32) * 0.5).T.astype(BF)
    w2f = w2[...].astype(F32)
    w2h = (w2f * 0.5).T.astype(BF)
    w2b = (w2f * 0.5).astype(BF)
    wo_row = wo[...].astype(F32)
    wo_col = jnp.broadcast_to(wo_row, (128, hid)).T
    wide_wo[0] = wo_col
    wide_wo[1] = 0.5 * wo_col
    sub = lax.broadcasted_iota(jnp.int32, (8, 128), 0)
    acc_second[...] = jnp.zeros_like(acc_second)
    acc_first[...] = jnp.zeros_like(acc_first)
    acc_outg[...] = jnp.zeros_like(acc_outg)

    def prepare(i, c):
        r0 = pl.multiple_of(i * 16, 16)
        x3 = jnp.swapaxes(drv[0, :, pl.ds(r0, 16), :].astype(F32), 0, 1).astype(BF)
        xs[:, pl.ds(pl.multiple_of(i * 2048, 2048), 2048)] = jnp.concatenate([x3[r] for r in range(16)], axis=1)
        return c
    lax.fori_loop(0, rows // 16, prepare, 0)
    ob = obs[0].astype(F32)
    mk = mask[...].astype(F32)
    wm = (conf[0].astype(F32) * mk).astype(BF).astype(F32)
    tg = ob * mk
    tgt_out[...] = tg
    obf[...] = ob
    wmf[...] = wm
    mkf[...] = mk

    def one(i, k, f1=True, f2=True, f3=True):
        a, b, c = k % 3, (k + 2) % 3, (k + 1) % 3
        n = wide // TILE
        if f3:
            x_old = xs[:, pl.ds(pl.multiple_of((i - 2) * wide, wide), wide)]
            d2 = d2s[c][...]
        if f1:
            x_new = xs[:, pl.ds(pl.multiple_of(jnp.minimum(i, units - 1) * wide, wide), wide)]
        def s3(j):
            sl = slice(j * TILE, (j + 1) * TILE)
            back = jnp.dot(w2b, d2[:, sl], preferred_element_type=F32)
            d1 = (back * s1s[c][:, sl]).astype(BF)
            acc_first[...] += lax.dot_general(d1, x_old[:, sl], NT, preferred_element_type=F32)
        def s1(j):
            sl = slice(j * TILE, (j + 1) * TILE)
            p1 = jnp.dot(w1h, x_new[:, sl], preferred_element_type=F32)
            t1 = jnp.tanh(p1)
            u1 = 1.0 + t1
            h1 = (p1 * u1).astype(BF)
            h1s[a][:, sl] = h1
            s1s[a][:, sl] = u1 * (1.0 + p1 * (1.0 - t1))
            p2s[a][:, sl] = jnp.dot(w2h, h1, preferred_element_type=F32)
        keep = []
        def s2(r):
            p2 = p2s[b][:, r * 128:(r + 1) * 128]
            t2 = jnp.tanh(p2)
            u2 = 1.0 + t2
            h2 = (p2 * u2).astype(BF)
            s2 = u2 * (1.0 + p2 * (1.0 - t2)) * wide_wo[1]
            keep.append((h2, s2))
        for r in range(8):
            if f2: s2(r)
            if r % (8 // n) == 0:
                if f1: s1(r // (8 // n))
                if f3: s3(r // (8 // n))
        if f3:
            acc_second[...] += lax.dot_general(h1s[c][...], d2, NT, preferred_element_type=F32)
        if not f2: return
        r0 = pl.multiple_of((i - 1) * UNIT, UNIT)
        h2w = jnp.concatenate([h for h, _ in keep], axis=1)
        scs = []
        for h2, _ in keep:
            sc = jnp.sum((h2.astype(F32) * wide_wo[0]).reshape(hid // 8, 8, 128), axis=0)
            for q in (4, 2, 1):
                sc = sc + pltpu.roll(sc, q, 0)
            scs.append(sc)
        score = scs[0]
        for r in range(1, 8):
            score = jnp.where(sub == r, scs[r], score)
        e = jnp.exp(-jnp.abs(score))
        imitated = jnp.maximum(score, 0.0) + jnp.log1p(e)
        sig = jnp.where(score >= 0, 1.0, e) / (1.0 + e)
        delta = wmf[pl.ds(r0, 8), :] * (imitated - obf[pl.ds(r0, 8), :]) * sig
        src_out[pl.ds(r0, 8), :] = mkf[pl.ds(r0, 8), :] * imitated
        mix = []
        high = delta.astype(BF).astype(F32)
        low = delta - high
        for r in range(8):
            h2, s2v = keep[r]
            d8 = jnp.broadcast_to(delta[r:r + 1], (8, 128))
            d = jnp.broadcast_to(d8[None], (hid // 8, 8, 128)).reshape(hid, 128)
            d2s[b][:, r * 128:(r + 1) * 128] = (d * s2v).astype(BF)
            mix.append(jnp.where(sub == 0, high[r:r + 1], jnp.where(sub == 1, low[r:r + 1], 0.0)))
        acc_outg[:, 0:8] += lax.dot_general(
            h2w, jnp.concatenate(mix, axis=1).astype(BF), NT, preferred_element_type=F32
        )

    one(0, 0, True, False, False)
    one(1, 1, True, True, False)
    def body(t, c):
        for k in range(3):
            one(t * 3 + 2 + k, 2 + k)
        return c
    loops = (units - 1 + 2) // 3
    lax.fori_loop(0, loops, body, 0)
    assert loops * 3 + 1 == units
    one(units + 1, units + 1, False, False, True)

    src = src_out[...]
    og = jnp.sum(acc_outg[...].T, axis=0, keepdims=True)
    me = lax.axis_index("maps")
    tot = lambda v: jnp.sum(jnp.sum(v, axis=1, keepdims=True), axis=0, keepdims=True)
    extra = jnp.where(sub == 0, og, 0.0)
    extra = jnp.where(sub == 1, tot(wmf[...]), extra)
    extra = jnp.where(sub == 2 + me, tot(src), extra)
    extra = jnp.where(sub == 4 + me, tot(tgt_out[...]), extra)
    second = acc_second[...]
    cut = hid // 2
    upper = jnp.concatenate([second[0:cut], extra, jnp.zeros((feat - 8, 128), F32)], axis=0)
    lower = jnp.concatenate([second[cut:hid], acc_first[...].T], axis=0)
    keep_out[...] = jnp.where(me == 0, upper, lower)
    send_out[...] = jnp.where(me == 0, lower, upper)
    if sides:
        lanes = lax.broadcasted_iota(jnp.int32, (rows, 128), 1)
        left, right = edge_strips(src, tgt_out[...], lanes)
        strips = [right, left]
        if sides == 1:
            strips = [jnp.where(lax.axis_index("cols") == 0, right, left)]
        for ref, strip in zip(strip_outs, strips):
            ref[...] = strip.astype(BF)


def vmem(*shape, dtype=F32):
    return pltpu.VMEM(shape, dtype)


def here(*values):
    return [pltpu.with_memory_space_constraint(value, pltpu.VMEM) for value in values]


PARAMS = pltpu.CompilerParams(vmem_limit_bytes=24 << 20)


def net(drivers, observed, confidence, land_mask, w1, w2, wo, sides):
    feat, hid = w1.shape
    rows, cols = land_mask.shape
    wide = UNIT * cols
    given = (drivers, observed, confidence, land_mask, w1, w2, wo.reshape(1, hid))
    return pl.pallas_call(
        functools.partial(net_kernel, sides),
        out_shape=[vmem(hid // 2 + feat, 128)] * 2
        + [vmem(rows, cols)] * 2
        + [vmem(rows, cols, dtype=BF)] * sides,
        scratch_shapes=[vmem(hid, wide, dtype=BF)] * 3
        + [vmem(hid, wide)] * 6
        + [vmem(hid, wide, dtype=BF)] * 3
        + [vmem(feat, rows * cols, dtype=BF)]
        + [vmem(rows, cols)] * 3
        + [vmem(hid, hid), vmem(hid, feat), vmem(hid, 128), vmem(2, hid, 128)]
        + [vmem(*value.shape, dtype=value.dtype) for value in given]
        + [pltpu.SemaphoreType.DMA((len(given),))],
        in_specs=[pl.BlockSpec(memory_space=pl.ANY)] * len(given),
        compiler_params=PARAMS,
        name="net",
    )(*[pltpu.with_memory_space_constraint(value, pltpu.HBM) for value in given])


def edge_strips(src, tgt, lane):
    right = jnp.where(lane >= 128 - 3 * RADIUS, src, pltpu.roll(tgt, 2 * RADIUS, 1))
    left = jnp.where(lane < 3 * RADIUS, src, pltpu.roll(tgt, 128 - 2 * RADIUS, 1))
    return left, right


def widen(src, tgt, strips):
    if not strips:
        return src, tgt
    lane = lax.broadcasted_iota(jnp.int32, src.shape, 1)
    first, last = strips[0][...].astype(F32), strips[-1][...].astype(F32)
    ls = jnp.where(lane >= 128 - 3 * RADIUS, first, 0.0)
    lt = jnp.where(lane >= 128 - 2 * RADIUS, pltpu.roll(first, 128 - 2 * RADIUS, 1), 0.0)
    rs = jnp.where(lane < 3 * RADIUS, last, 0.0)
    rt = jnp.where(lane < 2 * RADIUS, pltpu.roll(last, 2 * RADIUS, 1), 0.0)
    if len(strips) == 2:
        return jnp.concatenate([ls, src, rs], axis=1), jnp.concatenate([lt, tgt, rt], axis=1)
    at_left = lax.axis_index("cols") == 0
    return (
        jnp.concatenate([jnp.where(at_left, src, ls), jnp.where(at_left, rs, src)], axis=1),
        jnp.concatenate([jnp.where(at_left, tgt, lt), jnp.where(at_left, rt, tgt)], axis=1),
    )


def halo_kernel(src_ref, tgt_ref, *refs):
    strips, (up_ref, down_ref) = refs[:-2], refs[-2:]
    src, tgt = widen(src_ref[...], tgt_ref[...], strips)
    rows = src.shape[0]
    far, near = rows - 2 * RADIUS, 2 * RADIUS
    up_ref[...] = jnp.concatenate([src[0:far], tgt[0:near]], axis=0).astype(BF)
    down_ref[...] = jnp.concatenate([src[rows - far:], tgt[rows - near:]], axis=0).astype(BF)


def halo(src, tgt, strips):
    rows, cols = src.shape
    return pl.pallas_call(
        halo_kernel,
        out_shape=[vmem(rows, cols * (1 + len(strips)), dtype=BF)] * 2,
        compiler_params=PARAMS,
        name="halo",
    )(*here(src, tgt, *strips))


def parts(value):
    high = value.astype(BF)
    return high, (value - high.astype(F32)).astype(BF)


def product(left, right):
    (lh, ll), (rh, rl) = left, right
    dot = functools.partial(jnp.dot, preferred_element_type=F32)
    return dot(lh, rh) + (dot(lh, rl) + dot(ll, rh))


def sinkhorn_kernel(src_ref, tgt_ref, above_ref, below_ref, brow_ref, bcol_ref, krow_ref, kcol_ref, *refs):
    strips = refs[:-2]
    source_out, target_out = refs[-2:]
    sides = len(strips)
    far, near = 3 * RADIUS, 2 * RADIUS
    rows, wide = above_ref.shape
    rows_at, cols_at = lax.axis_index("rows"), lax.axis_index("cols")
    row_end, col_end = lax.axis_size("rows") - 1, lax.axis_size("cols") - 1
    src, tgt = widen(src_ref[...], tgt_ref[...], strips)
    above, below = above_ref[...].astype(F32), below_ref[...].astype(F32)
    source = jnp.concatenate([above[rows - near - far:rows - near], src, below[0:far]], axis=0)
    target = jnp.concatenate([above[rows - near:], tgt, below[rows - near:]], axis=0)
    own = (0, cols_at * 128, 128)[sides]

    def background(field, reach):
        row = lax.broadcasted_iota(jnp.int32, field.shape, 0)
        lane = lax.broadcasted_iota(jnp.int32, field.shape, 1)
        inside = (row >= jnp.where(rows_at == 0, reach, 0)) & (
            row < jnp.where(rows_at == row_end, reach + rows, 2 * reach + rows)
        )
        if sides:
            inside &= (lane >= own - jnp.where(cols_at == 0, 0, reach)) & (
                lane < own + 128 + jnp.where(cols_at == col_end, 0, reach)
            )
        return jnp.where(inside, field + BACKGROUND, 0.0)

    source, target = background(source, far), background(target, near)
    krow = 1.0 - (rows_at == 0).astype(F32) * krow_ref[0] - (rows_at == row_end).astype(F32) * krow_ref[1]
    if sides == 2:
        col_first, col_last = (cols_at == 0).astype(F32), (cols_at == col_end).astype(F32)
        kcol = 1.0 - col_first * kcol_ref[0:1, :] - col_last * kcol_ref[1:2, :]
    else:
        kcol = 1.0 - kcol_ref[0:1, :] - kcol_ref[1:2, :]
    krow = jnp.concatenate([krow] * (1 + sides), axis=1)
    brow = (brow_ref[0], brow_ref[1])
    bcol = (bcol_ref[0], bcol_ref[1])
    if sides == 1:
        last_bcol = tuple(jnp.where(cols_at == 0, band[:, 0:128], band[:, 128:256]) for band in bcol)
    else:
        last_bcol = tuple(band[:, own:own + 128] for band in bcol)

    def smooth(field, count, columns):
        bands = tuple(band[0:count, 0:count + near] for band in brow)
        return product(parts(product(bands, parts(field))), columns)

    def ratio(top, bottom):
        inside = top > 0.0
        return jnp.where(inside, top / jnp.where(inside, bottom, 1.0), 0.0)

    scaling = source / (krow * kcol)
    scaling = ratio(target, smooth(scaling, rows + 2 * near, bcol))
    scaling = ratio(source[near:near + rows + near], smooth(scaling, rows + near, bcol))
    bottom = smooth(scaling, rows, last_bcol)
    middle = scaling[RADIUS:RADIUS + rows]
    if sides == 1:
        source_out[...] = jnp.where(cols_at == 0, middle[:, 0:128], middle[:, 128:256])
    else:
        source_out[...] = middle[:, own:own + 128]
    target_out[...] = (tgt_ref[...] + BACKGROUND) / bottom


def split_table(table):
    high = table.astype(ml_dtypes.bfloat16)
    low = (table - high.astype(np.float64)).astype(ml_dtypes.bfloat16)
    return np.stack([high, low])


def taps():
    offsets = np.arange(-RADIUS, RADIUS + 1, dtype=np.float64)
    weights = np.exp(-4.5 * offsets * offsets / (RADIUS * RADIUS))
    return weights / weights.sum()


def tails(start, count, end):
    weights = taps()
    before, after = np.zeros(count), np.zeros(count)
    for at in range(count):
        if at >= start:
            before[at] = weights[: max(0, RADIUS - (at - start))].sum()
        if at < end:
            after[at] = weights[: max(0, RADIUS - (end - 1 - at))].sum()
    return np.stack([before, after])


def sinkhorn(src, tgt, above, below, strips):
    rows, cols = src.shape
    sides = len(strips)
    wide = cols * (1 + sides)
    weights = taps()

    def toeplitz(count_out, count_in, shift):
        offset = np.arange(count_in)[None, :] - np.arange(count_out)[:, None] + shift
        inside = (offset >= 0) & (offset <= 2 * RADIUS)
        return np.where(inside, weights[np.clip(offset, 0, 2 * RADIUS)], 0.0)

    brow = split_table(toeplitz(rows + 4 * RADIUS, rows + 6 * RADIUS, 0))
    bcol = split_table(toeplitz(wide, wide, RADIUS))
    krow = tails(3 * RADIUS, rows + 6 * RADIUS, 3 * RADIUS + rows)
    krow = np.broadcast_to(krow[:, :, None], krow.shape + (128,)).astype(np.float32)
    kcol = tails(cols, wide, 2 * cols) if sides == 2 else tails(0, wide, wide)
    kcol = np.concatenate([kcol, np.zeros((6, wide))]).astype(np.float32)
    tables = [jnp.asarray(table) for table in (brow, bcol, krow, kcol)]
    return pl.pallas_call(
        sinkhorn_kernel,
        out_shape=[vmem(rows, cols)] * 2,
        compiler_params=PARAMS,
        cost_estimate=pl.CostEstimate(flops=2000000000, bytes_accessed=1000000, transcendentals=0),
        name="sinkhorn",
    )(*here(src, tgt, above, below), *here(*tables), *here(*strips))


def finish_kernel(cells, hid, feat, mine_ref, other_ref, source_ref, target_ref, *outs):
    first_out, second_out, output_out, source_out, target_out = outs
    me = lax.axis_index("maps")
    mine, other = mine_ref[...], other_ref[...]
    upper, lower = jnp.where(me == 0, mine, other), jnp.where(me == 0, other, mine)
    cut = hid // 2
    tail = upper[cut:cut + 8]
    inverse = 1.0 / tail[1:2]
    second_out[0:cut, :] = upper[0:cut] * inverse
    second_out[cut:hid, :] = lower[0:cut] * inverse
    first_out[...] = lower[cut:cut + feat] * inverse
    output_out[...] = tail[0:1] * inverse
    source_mean = jnp.where(me == 0, tail[2:3], tail[3:4]) * (1.0 / cells) + BACKGROUND
    target_mean = jnp.where(me == 0, tail[4:5], tail[5:6]) * (1.0 / cells) + BACKGROUND
    ratio = source_mean / target_mean
    source_out[0] = source_ref[...] * (1.0 / (source_mean * ratio))
    target_out[0] = target_ref[...] * (ratio * ratio)


def finish(mine, other, source, target, cells, hid, feat):
    shape = jax.ShapeDtypeStruct((1,) + source.shape, F32)
    return pl.pallas_call(
        functools.partial(finish_kernel, cells, hid, feat),
        out_shape=(
            jax.ShapeDtypeStruct((feat, hid), F32),
            jax.ShapeDtypeStruct((hid, hid), F32),
            jax.ShapeDtypeStruct((1, hid), F32),
            shape,
            shape,
        ),
        compiler_params=PARAMS,
        name="finish",
    )(*here(mine, other, source, target))


def swap(value, axis, step):
    return lax.ppermute(value, axis, [(i, i ^ step) for i in range(lax.axis_size(axis))])


def shift(value, axis, step):
    count = lax.axis_size(axis)
    pairs = [(i, i + step) for i in range(count) if 0 <= i + step < count]
    return lax.ppermute(value, axis, pairs)


def powers(axis):
    return [1 << k for k in range((lax.axis_size(axis) - 1).bit_length())]


def local(
    drivers, observed, confidence, land_mask, ownership, first_layer, second_layer, output_layer
):
    feat, hid = first_layer.shape
    row_count, col_count = lax.axis_size("rows"), lax.axis_size("cols")
    cells = land_mask.size * row_count * col_count
    sides = min(col_count - 1, 2)
    keep, send, src, tgt, *strips = net(
        drivers, observed, confidence, land_mask, first_layer, second_layer, output_layer, sides
    )
    total = keep + swap(send, "maps", 1)
    if sides == 1:
        strips = [swap(strips[0], "cols", 1)]
    elif sides == 2:
        strips = [shift(strips[0], "cols", 1), shift(strips[1], "cols", -1)]
    for step in powers("cols"):
        total = total + swap(total, "cols", step)
    total, src, tgt, *strips = lax.optimization_barrier((total, src, tgt, *strips))
    up, down = halo(src, tgt, strips)
    above, below = shift(down, "rows", 1), shift(up, "rows", -1)
    for at, step in enumerate(powers("rows")):
        total = total + swap(total, "rows", step)
        if at == 0:
            total, above, below = lax.optimization_barrier((total, above, below))
    source, target = sinkhorn(src, tgt, above, below, strips)
    other = swap(total, "maps", 1)
    first, second, output, source, target = finish(total, other, source, target, cells, hid, feat)
    return first, second, output.reshape(hid), source, target


def solution(mesh):
    in_specs = (
        P(("groups", "maps"), None, "rows", "cols"),
        P(("groups", "maps"), "rows", "cols"),
        P(("groups", "maps"), "rows", "cols"),
        P(("groups", "rows"), "cols"),
        P(("groups", "rows"), "cols"),
        P(),
        P(),
        P(),
    )
    out_specs = (
        P("groups", None),
        P("groups", None),
        P("groups"),
        P(("groups", "maps"), "rows", "cols"),
        P(("groups", "maps"), "rows", "cols"),
    )
    return jax.shard_map(local, mesh=mesh, in_specs=in_specs, out_specs=out_specs, check_vma=False)
```

```python
import functools

import jax
import jax.numpy as jnp
import ml_dtypes
import numpy as np
from jax import lax
from jax.experimental import pallas as pl
from jax.experimental.pallas import tpu as pltpu
from jax.sharding import PartitionSpec as P

RADIUS = 24
BACKGROUND = 0.1
UNIT = 8
F32 = jnp.float32
BF = jnp.bfloat16
NT = (((1,), (1,)), ((), ()))


def net_kernel(sides, *refs):
    inputs, refs = refs[0:7], refs[7:]
    keep_out, send_out, src_out, tgt_out = refs[0:4]
    strip_outs, scr = refs[4:4 + sides], refs[4 + sides:]
    held, arrived, scr = scr[-8:-1], scr[-1], scr[:-8]
    copies = [pltpu.make_async_copy(a, b, arrived.at[k]) for k, (a, b) in enumerate(zip(inputs, held))]
    for copy in copies:
        copy.start()
    drv, obs, conf, mask, w1, w2, wo = held
    for copy in copies:
        copy.wait()
    rows = mask.shape[0]
    hid = w2.shape[0]
    feat = w1.shape[0]
    units = rows // UNIT
    wide = UNIT * 128
    TILE = 256
    h1s, s1s, p2s, d2s = scr[0:3], scr[3:6], scr[6:9], scr[9:12]
    xs, obf, wmf, mkf, acc_second, acc_first, acc_outg, wide_wo = scr[12:]
    w1h = (w1[...].astype(F32) * 0.5).T.astype(BF)
    w2f = w2[...].astype(F32)
    w2h = (w2f * 0.5).T.astype(BF)
    w2b = (w2f * 0.5).astype(BF)
    wo_row = wo[...].astype(F32)
    wo_col = jnp.broadcast_to(wo_row, (128, hid)).T
    wide_wo[0] = wo_col
    wide_wo[1] = 0.5 * wo_col
    sub = lax.broadcasted_iota(jnp.int32, (8, 128), 0)
    acc_second[...] = jnp.zeros_like(acc_second)
    acc_first[...] = jnp.zeros_like(acc_first)
    acc_outg[...] = jnp.zeros_like(acc_outg)

    def prepare(i, c):
        r0 = pl.multiple_of(i * 16, 16)
        x3 = jnp.swapaxes(drv[0, :, pl.ds(r0, 16), :].astype(F32), 0, 1).astype(BF)
        xs[:, pl.ds(pl.multiple_of(i * 2048, 2048), 2048)] = jnp.concatenate([x3[r] for r in range(16)], axis=1)
        return c
    lax.fori_loop(0, rows // 16, prepare, 0)
    ob = obs[0].astype(F32)
    mk = mask[...].astype(F32)
    wm = (conf[0].astype(F32) * mk).astype(BF).astype(F32)
    tg = ob * mk
    tgt_out[...] = tg
    obf[...] = ob
    wmf[...] = wm
    mkf[...] = mk

    def one(i, k, f1=True, f2=True, f3=True):
        a, b, c = k % 3, (k + 2) % 3, (k + 1) % 3
        n = wide // TILE
        if f3:
            x_old = xs[:, pl.ds(pl.multiple_of((i - 2) * wide, wide), wide)]
            d2 = d2s[c][...]
        if f1:
            x_new = xs[:, pl.ds(pl.multiple_of(jnp.minimum(i, units - 1) * wide, wide), wide)]
        def s3(j):
            sl = slice(j * TILE, (j + 1) * TILE)
            back = jnp.dot(w2b, d2[:, sl], preferred_element_type=F32)
            d1 = (back * s1s[c][:, sl]).astype(BF)
            acc_first[...] += lax.dot_general(d1, x_old[:, sl], NT, preferred_element_type=F32)
        def s1(j):
            sl = slice(j * TILE, (j + 1) * TILE)
            p1 = jnp.dot(w1h, x_new[:, sl], preferred_element_type=F32)
            t1 = jnp.tanh(p1)
            u1 = 1.0 + t1
            h1 = (p1 * u1).astype(BF)
            h1s[a][:, sl] = h1
            s1s[a][:, sl] = u1 * (1.0 + p1 * (1.0 - t1))
            p2s[a][:, sl] = jnp.dot(w2h, h1, preferred_element_type=F32)
        keep = []
        def s2(r):
            p2 = p2s[b][:, r * 128:(r + 1) * 128]
            t2 = jnp.tanh(p2)
            u2 = 1.0 + t2
            h2 = (p2 * u2).astype(BF)
            s2 = u2 * (1.0 + p2 * (1.0 - t2)) * wide_wo[1]
            keep.append((h2, s2))
        for r in range(8):
            if f2: s2(r)
            if r % (8 // n) == 0:
                if f1: s1(r // (8 // n))
                if f3: s3(r // (8 // n))
        if f3:
            acc_second[...] += lax.dot_general(h1s[c][...], d2, NT, preferred_element_type=F32)
        if not f2: return
        r0 = pl.multiple_of((i - 1) * UNIT, UNIT)
        h2w = jnp.concatenate([h for h, _ in keep], axis=1)
        scs = []
        for h2, _ in keep:
            sc = jnp.sum((h2.astype(F32) * wide_wo[0]).reshape(hid // 8, 8, 128), axis=0)
            for q in (4, 2, 1):
                sc = sc + pltpu.roll(sc, q, 0)
            scs.append(sc)
        score = scs[0]
        for r in range(1, 8):
            score = jnp.where(sub == r, scs[r], score)
        e = jnp.exp(-jnp.abs(score))
        imitated = jnp.maximum(score, 0.0) + jnp.log1p(e)
        sig = jnp.where(score >= 0, 1.0, e) / (1.0 + e)
        delta = wmf[pl.ds(r0, 8), :] * (imitated - obf[pl.ds(r0, 8), :]) * sig
        src_out[pl.ds(r0, 8), :] = mkf[pl.ds(r0, 8), :] * imitated
        mix = []
        high = delta.astype(BF).astype(F32)
        low = delta - high
        for r in range(8):
            h2, s2v = keep[r]
            d8 = jnp.broadcast_to(delta[r:r + 1], (8, 128))
            d = jnp.broadcast_to(d8[None], (hid // 8, 8, 128)).reshape(hid, 128)
            d2s[b][:, r * 128:(r + 1) * 128] = (d * s2v).astype(BF)
            mix.append(jnp.where(sub == 0, high[r:r + 1], jnp.where(sub == 1, low[r:r + 1], 0.0)))
        acc_outg[:, 0:8] += lax.dot_general(
            h2w, jnp.concatenate(mix, axis=1).astype(BF), NT, preferred_element_type=F32
        )

    one(0, 0, True, False, False)
    one(1, 1, True, True, False)
    def body(t, c):
        for k in range(3):
            one(t * 3 + 2 + k, 2 + k)
        return c
    loops = (units - 1 + 2) // 3
    lax.fori_loop(0, loops, body, 0)
    assert loops * 3 + 1 == units
    one(units + 1, units + 1, False, False, True)

    src = src_out[...]
    og = jnp.sum(acc_outg[...].T, axis=0, keepdims=True)
    me = lax.axis_index("maps")
    tot = lambda v: jnp.sum(jnp.sum(v, axis=1, keepdims=True), axis=0, keepdims=True)
    extra = jnp.where(sub == 0, og, 0.0)
    extra = jnp.where(sub == 1, tot(wmf[...]), extra)
    extra = jnp.where(sub == 2 + me, tot(src), extra)
    extra = jnp.where(sub == 4 + me, tot(tgt_out[...]), extra)
    second = acc_second[...]
    cut = hid // 2
    upper = jnp.concatenate([second[0:cut], extra, jnp.zeros((feat - 8, 128), F32)], axis=0)
    lower = jnp.concatenate([second[cut:hid], acc_first[...].T], axis=0)
    keep_out[...] = jnp.where(me == 0, upper, lower)
    send_out[...] = jnp.where(me == 0, lower, upper)
    if sides:
        lanes = lax.broadcasted_iota(jnp.int32, (rows, 128), 1)
        left, right = edge_strips(src, tgt_out[...], lanes)
        strips = [right, left]
        if sides == 1:
            strips = [jnp.where(lax.axis_index("cols") == 0, right, left)]
        for ref, strip in zip(strip_outs, strips):
            ref[...] = strip.astype(BF)


def vmem(*shape, dtype=F32):
    return pltpu.VMEM(shape, dtype)


def here(*values):
    return [pltpu.with_memory_space_constraint(value, pltpu.VMEM) for value in values]


PARAMS = pltpu.CompilerParams(vmem_limit_bytes=24 << 20)


def net(drivers, observed, confidence, land_mask, w1, w2, wo, sides):
    feat, hid = w1.shape
    rows, cols = land_mask.shape
    wide = UNIT * cols
    given = (drivers, observed, confidence, land_mask, w1, w2, wo.reshape(1, hid))
    return pl.pallas_call(
        functools.partial(net_kernel, sides),
        out_shape=[vmem(hid // 2 + feat, 128)] * 2
        + [vmem(rows, cols)] * 2
        + [vmem(rows, cols, dtype=BF)] * sides,
        scratch_shapes=[vmem(hid, wide, dtype=BF)] * 3
        + [vmem(hid, wide)] * 6
        + [vmem(hid, wide, dtype=BF)] * 3
        + [vmem(feat, rows * cols, dtype=BF)]
        + [vmem(rows, cols)] * 3
        + [vmem(hid, hid), vmem(hid, feat), vmem(hid, 128), vmem(2, hid, 128)]
        + [vmem(*value.shape, dtype=value.dtype) for value in given]
        + [pltpu.SemaphoreType.DMA((len(given),))],
        in_specs=[pl.BlockSpec(memory_space=pl.ANY)] * len(given),
        compiler_params=PARAMS,
        name="net",
    )(*[pltpu.with_memory_space_constraint(value, pltpu.HBM) for value in given])


def edge_strips(src, tgt, lane):
    right = jnp.where(lane >= 128 - 3 * RADIUS, src, pltpu.roll(tgt, 2 * RADIUS, 1))
    left = jnp.where(lane < 3 * RADIUS, src, pltpu.roll(tgt, 128 - 2 * RADIUS, 1))
    return left, right


def widen(src, tgt, strips):
    if not strips:
        return src, tgt
    lane = lax.broadcasted_iota(jnp.int32, src.shape, 1)
    first, last = strips[0][...].astype(F32), strips[-1][...].astype(F32)
    ls = jnp.where(lane >= 128 - 3 * RADIUS, first, 0.0)
    lt = jnp.where(lane >= 128 - 2 * RADIUS, pltpu.roll(first, 128 - 2 * RADIUS, 1), 0.0)
    rs = jnp.where(lane < 3 * RADIUS, last, 0.0)
    rt = jnp.where(lane < 2 * RADIUS, pltpu.roll(last, 2 * RADIUS, 1), 0.0)
    if len(strips) == 2:
        return jnp.concatenate([ls, src, rs], axis=1), jnp.concatenate([lt, tgt, rt], axis=1)
    at_left = lax.axis_index("cols") == 0
    return (
        jnp.concatenate([jnp.where(at_left, src, ls), jnp.where(at_left, rs, src)], axis=1),
        jnp.concatenate([jnp.where(at_left, tgt, lt), jnp.where(at_left, rt, tgt)], axis=1),
    )


def halo_kernel(src_ref, tgt_ref, *refs):
    strips, (near_ref, far_ref) = refs[:-2], refs[-2:]
    src, tgt = widen(src_ref[...], tgt_ref[...], strips)
    rows = src.shape[0]
    far, near = rows - 2 * RADIUS, 2 * RADIUS
    up = jnp.concatenate([src[0:far], tgt[0:near]], axis=0)
    down = jnp.concatenate([src[rows - far:], tgt[rows - near:]], axis=0)
    even = lax.axis_index("rows") % 2 == 0
    near_ref[...] = jnp.where(even, down, up).astype(BF)
    far_ref[...] = jnp.where(even, up, down).astype(BF)


def halo(src, tgt, strips):
    rows, cols = src.shape
    return pl.pallas_call(
        halo_kernel,
        out_shape=[vmem(rows, cols * (1 + len(strips)), dtype=BF)] * 2,
        compiler_params=PARAMS,
        name="halo",
    )(*here(src, tgt, *strips))


def parts(value):
    high = value.astype(BF)
    return high, (value - high.astype(F32)).astype(BF)


def product(left, right):
    (lh, ll), (rh, rl) = left, right
    dot = functools.partial(jnp.dot, preferred_element_type=F32)
    return dot(lh, rh) + (dot(lh, rl) + dot(ll, rh))


def sinkhorn_kernel(src_ref, tgt_ref, pair_ref, next_ref, brow_ref, bcol_ref, krow_ref, kcol_ref, *refs):
    strips = refs[:-2]
    source_out, target_out = refs[-2:]
    sides = len(strips)
    far, near = 3 * RADIUS, 2 * RADIUS
    rows, wide = pair_ref.shape
    rows_at, cols_at = lax.axis_index("rows"), lax.axis_index("cols")
    row_end, col_end = lax.axis_size("rows") - 1, lax.axis_size("cols") - 1
    src, tgt = widen(src_ref[...], tgt_ref[...], strips)
    pair, following = pair_ref[...].astype(F32), next_ref[...].astype(F32)
    even = rows_at % 2 == 0
    above, below = jnp.where(even, following, pair), jnp.where(even, pair, following)
    source = jnp.concatenate([above[rows - near - far:rows - near], src, below[0:far]], axis=0)
    target = jnp.concatenate([above[rows - near:], tgt, below[rows - near:]], axis=0)
    own = (0, cols_at * 128, 128)[sides]

    def background(field, reach):
        row = lax.broadcasted_iota(jnp.int32, field.shape, 0)
        lane = lax.broadcasted_iota(jnp.int32, field.shape, 1)
        inside = (row >= jnp.where(rows_at == 0, reach, 0)) & (
            row < jnp.where(rows_at == row_end, reach + rows, 2 * reach + rows)
        )
        if sides:
            inside &= (lane >= own - jnp.where(cols_at == 0, 0, reach)) & (
                lane < own + 128 + jnp.where(cols_at == col_end, 0, reach)
            )
        return jnp.where(inside, field + BACKGROUND, 0.0)

    source, target = background(source, far), background(target, near)
    krow = 1.0 - (rows_at == 0).astype(F32) * krow_ref[0] - (rows_at == row_end).astype(F32) * krow_ref[1]
    if sides == 2:
        col_first, col_last = (cols_at == 0).astype(F32), (cols_at == col_end).astype(F32)
        kcol = 1.0 - col_first * kcol_ref[0:1, :] - col_last * kcol_ref[1:2, :]
    else:
        kcol = 1.0 - kcol_ref[0:1, :] - kcol_ref[1:2, :]
    krow = jnp.concatenate([krow] * (1 + sides), axis=1)
    brow = (brow_ref[0], brow_ref[1])
    bcol = (bcol_ref[0], bcol_ref[1])
    if sides == 1:
        last_bcol = tuple(jnp.where(cols_at == 0, band[:, 0:128], band[:, 128:256]) for band in bcol)
    else:
        last_bcol = tuple(band[:, own:own + 128] for band in bcol)

    def smooth(field, count, columns):
        bands = tuple(band[0:count, 0:count + near] for band in brow)
        return product(parts(product(bands, parts(field))), columns)

    def ratio(top, bottom):
        inside = top > 0.0
        return jnp.where(inside, top / jnp.where(inside, bottom, 1.0), 0.0)

    scaling = source / (krow * kcol)
    scaling = ratio(target, smooth(scaling, rows + 2 * near, bcol))
    scaling = ratio(source[near:near + rows + near], smooth(scaling, rows + near, bcol))
    bottom = smooth(scaling, rows, last_bcol)
    middle = scaling[RADIUS:RADIUS + rows]
    if sides == 1:
        source_out[...] = jnp.where(cols_at == 0, middle[:, 0:128], middle[:, 128:256])
    else:
        source_out[...] = middle[:, own:own + 128]
    target_out[...] = (tgt_ref[...] + BACKGROUND) / bottom


def split_table(table):
    high = table.astype(ml_dtypes.bfloat16)
    low = (table - high.astype(np.float64)).astype(ml_dtypes.bfloat16)
    return np.stack([high, low])


def taps():
    offsets = np.arange(-RADIUS, RADIUS + 1, dtype=np.float64)
    weights = np.exp(-4.5 * offsets * offsets / (RADIUS * RADIUS))
    return weights / weights.sum()


def tails(start, count, end):
    weights = taps()
    before, after = np.zeros(count), np.zeros(count)
    for at in range(count):
        if at >= start:
            before[at] = weights[: max(0, RADIUS - (at - start))].sum()
        if at < end:
            after[at] = weights[: max(0, RADIUS - (end - 1 - at))].sum()
    return np.stack([before, after])


def sinkhorn(src, tgt, pair, following, strips):
    rows, cols = src.shape
    sides = len(strips)
    wide = cols * (1 + sides)
    weights = taps()

    def toeplitz(count_out, count_in, shift):
        offset = np.arange(count_in)[None, :] - np.arange(count_out)[:, None] + shift
        inside = (offset >= 0) & (offset <= 2 * RADIUS)
        return np.where(inside, weights[np.clip(offset, 0, 2 * RADIUS)], 0.0)

    brow = split_table(toeplitz(rows + 4 * RADIUS, rows + 6 * RADIUS, 0))
    bcol = split_table(toeplitz(wide, wide, RADIUS))
    krow = tails(3 * RADIUS, rows + 6 * RADIUS, 3 * RADIUS + rows)
    krow = np.broadcast_to(krow[:, :, None], krow.shape + (128,)).astype(np.float32)
    kcol = tails(cols, wide, 2 * cols) if sides == 2 else tails(0, wide, wide)
    kcol = np.concatenate([kcol, np.zeros((6, wide))]).astype(np.float32)
    tables = [jnp.asarray(table) for table in (brow, bcol, krow, kcol)]
    return pl.pallas_call(
        sinkhorn_kernel,
        out_shape=[vmem(rows, cols)] * 2,
        compiler_params=PARAMS,
        cost_estimate=pl.CostEstimate(flops=2000000000, bytes_accessed=1000000, transcendentals=0),
        name="sinkhorn",
    )(*here(src, tgt, pair, following), *here(*tables), *here(*strips))


def finish_kernel(cells, hid, feat, mine_ref, other_ref, source_ref, target_ref, *outs):
    first_out, second_out, output_out, source_out, target_out = outs
    me = lax.axis_index("maps")
    mine, other = mine_ref[...], other_ref[...]
    upper, lower = jnp.where(me == 0, mine, other), jnp.where(me == 0, other, mine)
    cut = hid // 2
    tail = upper[cut:cut + 8]
    inverse = 1.0 / tail[1:2]
    second_out[0:cut, :] = upper[0:cut] * inverse
    second_out[cut:hid, :] = lower[0:cut] * inverse
    first_out[...] = lower[cut:cut + feat] * inverse
    output_out[...] = tail[0:1] * inverse
    source_mean = jnp.where(me == 0, tail[2:3], tail[3:4]) * (1.0 / cells) + BACKGROUND
    target_mean = jnp.where(me == 0, tail[4:5], tail[5:6]) * (1.0 / cells) + BACKGROUND
    ratio = source_mean / target_mean
    source_out[0] = source_ref[...] * (1.0 / (source_mean * ratio))
    target_out[0] = target_ref[...] * (ratio * ratio)


def finish(mine, other, source, target, cells, hid, feat):
    shape = jax.ShapeDtypeStruct((1,) + source.shape, F32)
    return pl.pallas_call(
        functools.partial(finish_kernel, cells, hid, feat),
        out_shape=(
            jax.ShapeDtypeStruct((feat, hid), F32),
            jax.ShapeDtypeStruct((hid, hid), F32),
            jax.ShapeDtypeStruct((1, hid), F32),
            shape,
            shape,
        ),
        compiler_params=PARAMS,
        name="finish",
    )(*here(mine, other, source, target))


def swap(value, axis, step):
    return lax.ppermute(value, axis, [(i, i ^ step) for i in range(lax.axis_size(axis))])


def shift(value, axis, step):
    count = lax.axis_size(axis)
    pairs = [(i, i + step) for i in range(count) if 0 <= i + step < count]
    return lax.ppermute(value, axis, pairs)


def exchange(value, axis, start):
    count = lax.axis_size(axis)
    pairs = [pair for i in range(start, count - 1, 2) for pair in ((i, i + 1), (i + 1, i))]
    return lax.ppermute(value, axis, pairs)


def powers(axis):
    return [1 << k for k in range((lax.axis_size(axis) - 1).bit_length())]


def local(
    drivers, observed, confidence, land_mask, ownership, first_layer, second_layer, output_layer
):
    feat, hid = first_layer.shape
    row_count, col_count = lax.axis_size("rows"), lax.axis_size("cols")
    cells = land_mask.size * row_count * col_count
    sides = min(col_count - 1, 2)
    keep, send, src, tgt, *strips = net(
        drivers, observed, confidence, land_mask, first_layer, second_layer, output_layer, sides
    )
    total = keep + swap(send, "maps", 1)
    if sides == 1:
        strips = [swap(strips[0], "cols", 1)]
    elif sides == 2:
        strips = [shift(strips[0], "cols", 1), shift(strips[1], "cols", -1)]
    for step in powers("cols"):
        total = total + swap(total, "cols", step)
    total, src, tgt, *strips = lax.optimization_barrier((total, src, tgt, *strips))
    to_pair, to_next = halo(src, tgt, strips)
    pair = exchange(to_pair, "rows", 0)
    for at, step in enumerate(powers("rows")):
        total = total + swap(total, "rows", 2 * step - 1)
        if at == 0:
            total, pair, to_next = lax.optimization_barrier((total, pair, to_next))
    following = exchange(to_next, "rows", 1)
    source, target = sinkhorn(src, tgt, pair, following, strips)
    other = swap(total, "maps", 1)
    first, second, output, source, target = finish(total, other, source, target, cells, hid, feat)
    return first, second, output.reshape(hid), source, target


def solution(mesh):
    in_specs = (
        P(("groups", "maps"), None, "rows", "cols"),
        P(("groups", "maps"), "rows", "cols"),
        P(("groups", "maps"), "rows", "cols"),
        P(("groups", "rows"), "cols"),
        P(("groups", "rows"), "cols"),
        P(),
        P(),
        P(),
    )
    out_specs = (
        P("groups", None),
        P("groups", None),
        P("groups"),
        P(("groups", "maps"), "rows", "cols"),
        P(("groups", "maps"), "rows", "cols"),
    )
    return jax.shard_map(local, mesh=mesh, in_specs=in_specs, out_specs=out_specs, check_vma=False)
```

```python
import functools

import jax
import jax.numpy as jnp
import ml_dtypes
import numpy as np
from jax import lax
from jax.experimental import pallas as pl
from jax.experimental.pallas import tpu as pltpu
from jax.sharding import PartitionSpec as P

RADIUS = 24
BACKGROUND = 0.1
UNIT = 8
F32 = jnp.float32
BF = jnp.bfloat16
NT = (((1,), (1,)), ((), ()))


def net_kernel(sides, *refs):
    inputs, refs = refs[0:7], refs[7:]
    keep_out, send_out, src_out, tgt_out = refs[0:4]
    strip_outs, scr = refs[4:4 + sides], refs[4 + sides:]
    held, arrived, scr = scr[-8:-1], scr[-1], scr[:-8]
    copies = [pltpu.make_async_copy(a, b, arrived.at[k]) for k, (a, b) in enumerate(zip(inputs, held))]
    for copy in copies:
        copy.start()
    drv, obs, conf, mask, w1, w2, wo = held
    for copy in copies:
        copy.wait()
    rows = mask.shape[0]
    hid = w2.shape[0]
    feat = w1.shape[0]
    units = rows // UNIT
    wide = UNIT * 128
    TILE = 256
    h1s, s1s, p2s, d2s = scr[0:3], scr[3:6], scr[6:9], scr[9:12]
    xs, obf, wmf, mkf, acc_second, acc_first, acc_outg, wide_wo = scr[12:]
    w1h = (w1[...].astype(F32) * 0.5).T.astype(BF)
    w2f = w2[...].astype(F32)
    w2h = (w2f * 0.5).T.astype(BF)
    w2b = (w2f * 0.5).astype(BF)
    wo_row = wo[...].astype(F32)
    wo_col = jnp.broadcast_to(wo_row, (128, hid)).T
    wide_wo[0] = wo_col
    wide_wo[1] = 0.5 * wo_col
    sub = lax.broadcasted_iota(jnp.int32, (8, 128), 0)
    acc_second[...] = jnp.zeros_like(acc_second)
    acc_first[...] = jnp.zeros_like(acc_first)
    acc_outg[...] = jnp.zeros_like(acc_outg)

    def prepare(i, c):
        r0 = pl.multiple_of(i * 16, 16)
        x3 = jnp.swapaxes(drv[0, :, pl.ds(r0, 16), :].astype(F32), 0, 1).astype(BF)
        xs[:, pl.ds(pl.multiple_of(i * 2048, 2048), 2048)] = jnp.concatenate([x3[r] for r in range(16)], axis=1)
        return c
    lax.fori_loop(0, rows // 16, prepare, 0)
    ob = obs[0].astype(F32)
    mk = mask[...].astype(F32)
    wm = (conf[0].astype(F32) * mk).astype(BF).astype(F32)
    tg = ob * mk
    tgt_out[...] = tg
    obf[...] = ob
    wmf[...] = wm
    mkf[...] = mk

    def one(i, k, f1=True, f2=True, f3=True):
        a, b, c = k % 3, (k + 2) % 3, (k + 1) % 3
        n = wide // TILE
        if f3:
            x_old = xs[:, pl.ds(pl.multiple_of((i - 2) * wide, wide), wide)]
            d2 = d2s[c][...]
        if f1:
            x_new = xs[:, pl.ds(pl.multiple_of(jnp.minimum(i, units - 1) * wide, wide), wide)]
        def s3(j):
            sl = slice(j * TILE, (j + 1) * TILE)
            back = jnp.dot(w2b, d2[:, sl], preferred_element_type=F32)
            d1 = (back * s1s[c][:, sl]).astype(BF)
            acc_first[...] += lax.dot_general(d1, x_old[:, sl], NT, preferred_element_type=F32)
        def s1(j):
            sl = slice(j * TILE, (j + 1) * TILE)
            p1 = jnp.dot(w1h, x_new[:, sl], preferred_element_type=F32)
            t1 = jnp.tanh(p1)
            u1 = 1.0 + t1
            h1 = (p1 * u1).astype(BF)
            h1s[a][:, sl] = h1
            s1s[a][:, sl] = u1 * (1.0 + p1 * (1.0 - t1))
            p2s[a][:, sl] = jnp.dot(w2h, h1, preferred_element_type=F32)
        keep = []
        def s2(r):
            p2 = p2s[b][:, r * 128:(r + 1) * 128]
            t2 = jnp.tanh(p2)
            u2 = 1.0 + t2
            h2 = (p2 * u2).astype(BF)
            s2 = u2 * (1.0 + p2 * (1.0 - t2)) * wide_wo[1]
            keep.append((h2, s2))
        for r in range(8):
            if f2: s2(r)
            if r % (8 // n) == 0:
                if f1: s1(r // (8 // n))
                if f3: s3(r // (8 // n))
        if f3:
            acc_second[...] += lax.dot_general(h1s[c][...], d2, NT, preferred_element_type=F32)
        if not f2: return
        r0 = pl.multiple_of((i - 1) * UNIT, UNIT)
        h2w = jnp.concatenate([h for h, _ in keep], axis=1)
        scs = []
        for h2, _ in keep:
            sc = jnp.sum((h2.astype(F32) * wide_wo[0]).reshape(hid // 8, 8, 128), axis=0)
            for q in (4, 2, 1):
                sc = sc + pltpu.roll(sc, q, 0)
            scs.append(sc)
        score = scs[0]
        for r in range(1, 8):
            score = jnp.where(sub == r, scs[r], score)
        e = jnp.exp(-jnp.abs(score))
        imitated = jnp.maximum(score, 0.0) + jnp.log1p(e)
        sig = jnp.where(score >= 0, 1.0, e) / (1.0 + e)
        delta = wmf[pl.ds(r0, 8), :] * (imitated - obf[pl.ds(r0, 8), :]) * sig
        src_out[pl.ds(r0, 8), :] = mkf[pl.ds(r0, 8), :] * imitated
        mix = []
        high = delta.astype(BF).astype(F32)
        low = delta - high
        for r in range(8):
            h2, s2v = keep[r]
            d8 = jnp.broadcast_to(delta[r:r + 1], (8, 128))
            d = jnp.broadcast_to(d8[None], (hid // 8, 8, 128)).reshape(hid, 128)
            d2s[b][:, r * 128:(r + 1) * 128] = (d * s2v).astype(BF)
            mix.append(jnp.where(sub == 0, high[r:r + 1], jnp.where(sub == 1, low[r:r + 1], 0.0)))
        acc_outg[:, 0:8] += lax.dot_general(
            h2w, jnp.concatenate(mix, axis=1).astype(BF), NT, preferred_element_type=F32
        )

    one(0, 0, True, False, False)
    one(1, 1, True, True, False)
    def body(t, c):
        for k in range(3):
            one(t * 3 + 2 + k, 2 + k)
        return c
    loops = (units - 1 + 2) // 3
    lax.fori_loop(0, loops, body, 0)
    assert loops * 3 + 1 == units
    one(units + 1, units + 1, False, False, True)

    src = src_out[...]
    og = jnp.sum(acc_outg[...].T, axis=0, keepdims=True)
    me = lax.axis_index("maps")
    tot = lambda v: jnp.sum(jnp.sum(v, axis=1, keepdims=True), axis=0, keepdims=True)
    extra = jnp.where(sub == 0, og, 0.0)
    extra = jnp.where(sub == 1, tot(wmf[...]), extra)
    extra = jnp.where(sub == 2 + me, tot(src), extra)
    extra = jnp.where(sub == 4 + me, tot(tgt_out[...]), extra)
    second = acc_second[...]
    cut = hid // 2
    upper = jnp.concatenate([second[0:cut], extra, jnp.zeros((feat - 8, 128), F32)], axis=0)
    lower = jnp.concatenate([second[cut:hid], acc_first[...].T], axis=0)
    keep_out[...] = jnp.where(me == 0, upper, lower)
    send_out[...] = jnp.where(me == 0, lower, upper)
    if sides:
        lanes = lax.broadcasted_iota(jnp.int32, (rows, 128), 1)
        left, right = edge_strips(src, tgt_out[...], lanes)
        strips = [right, left]
        if sides == 1:
            strips = [jnp.where(lax.axis_index("cols") == 0, right, left)]
        for ref, strip in zip(strip_outs, strips):
            ref[...] = strip


def vmem(*shape, dtype=F32):
    return pltpu.VMEM(shape, dtype)


def here(*values):
    return [pltpu.with_memory_space_constraint(value, pltpu.VMEM) for value in values]


PARAMS = pltpu.CompilerParams(vmem_limit_bytes=24 << 20)


def net(drivers, observed, confidence, land_mask, w1, w2, wo, sides):
    feat, hid = w1.shape
    rows, cols = land_mask.shape
    wide = UNIT * cols
    given = (drivers, observed, confidence, land_mask, w1, w2, wo.reshape(1, hid))
    return pl.pallas_call(
        functools.partial(net_kernel, sides),
        out_shape=[vmem(hid // 2 + feat, 128)] * 2
        + [vmem(rows, cols)] * 2
        + [vmem(rows, cols)] * sides,
        scratch_shapes=[vmem(hid, wide, dtype=BF)] * 3
        + [vmem(hid, wide)] * 6
        + [vmem(hid, wide, dtype=BF)] * 3
        + [vmem(feat, rows * cols, dtype=BF)]
        + [vmem(rows, cols)] * 3
        + [vmem(hid, hid), vmem(hid, feat), vmem(hid, 128), vmem(2, hid, 128)]
        + [vmem(*value.shape, dtype=value.dtype) for value in given]
        + [pltpu.SemaphoreType.DMA((len(given),))],
        in_specs=[pl.BlockSpec(memory_space=pl.ANY)] * len(given),
        compiler_params=PARAMS,
        name="net",
    )(*[pltpu.with_memory_space_constraint(value, pltpu.HBM) for value in given])


def edge_strips(src, tgt, lane):
    right = jnp.where(lane >= 128 - 3 * RADIUS, src, pltpu.roll(tgt, 2 * RADIUS, 1))
    left = jnp.where(lane < 3 * RADIUS, src, pltpu.roll(tgt, 128 - 2 * RADIUS, 1))
    return left, right


def widen(src, tgt, strips):
    if not strips:
        return src, tgt
    lane = lax.broadcasted_iota(jnp.int32, src.shape, 1)
    first, last = strips[0][...].astype(F32), strips[-1][...].astype(F32)
    ls = jnp.where(lane >= 128 - 3 * RADIUS, first, 0.0)
    lt = jnp.where(lane >= 128 - 2 * RADIUS, pltpu.roll(first, 128 - 2 * RADIUS, 1), 0.0)
    rs = jnp.where(lane < 3 * RADIUS, last, 0.0)
    rt = jnp.where(lane < 2 * RADIUS, pltpu.roll(last, 2 * RADIUS, 1), 0.0)
    if len(strips) == 2:
        return jnp.concatenate([ls, src, rs], axis=1), jnp.concatenate([lt, tgt, rt], axis=1)
    at_left = lax.axis_index("cols") == 0
    return (
        jnp.concatenate([jnp.where(at_left, src, ls), jnp.where(at_left, rs, src)], axis=1),
        jnp.concatenate([jnp.where(at_left, tgt, lt), jnp.where(at_left, rt, tgt)], axis=1),
    )


def halo_kernel(src_ref, tgt_ref, *refs):
    strips, (near_ref, far_ref) = refs[:-2], refs[-2:]
    src, tgt = widen(src_ref[...], tgt_ref[...], strips)
    rows = src.shape[0]
    far, near = rows - 2 * RADIUS, 2 * RADIUS
    up = jnp.concatenate([src[0:far], tgt[0:near]], axis=0)
    down = jnp.concatenate([src[rows - far:], tgt[rows - near:]], axis=0)
    even = lax.axis_index("rows") % 2 == 0
    near_ref[...] = jnp.where(even, down, up).astype(BF)
    far_ref[...] = jnp.where(even, up, down).astype(BF)


def halo(src, tgt, strips):
    rows, cols = src.shape
    return pl.pallas_call(
        halo_kernel,
        out_shape=[vmem(rows, cols * (1 + len(strips)), dtype=BF)] * 2,
        compiler_params=PARAMS,
        name="halo",
    )(*here(src, tgt, *strips))


def parts(value):
    high = value.astype(BF)
    return high, (value - high.astype(F32)).astype(BF)


def product(left, right):
    (lh, ll), (rh, rl) = left, right
    dot = functools.partial(jnp.dot, preferred_element_type=F32)
    return dot(lh, rh) + (dot(lh, rl) + dot(ll, rh))


def sinkhorn_kernel(src_ref, tgt_ref, pair_ref, next_ref, brow_ref, bcol_ref, krow_ref, kcol_ref, *refs):
    strips = refs[:-2]
    source_out, target_out = refs[-2:]
    sides = len(strips)
    far, near = 3 * RADIUS, 2 * RADIUS
    rows, wide = pair_ref.shape
    rows_at, cols_at = lax.axis_index("rows"), lax.axis_index("cols")
    row_end, col_end = lax.axis_size("rows") - 1, lax.axis_size("cols") - 1
    src, tgt = widen(src_ref[...], tgt_ref[...], strips)
    pair, following = pair_ref[...].astype(F32), next_ref[...].astype(F32)
    even = rows_at % 2 == 0
    above, below = jnp.where(even, following, pair), jnp.where(even, pair, following)
    source = jnp.concatenate([above[rows - near - far:rows - near], src, below[0:far]], axis=0)
    target = jnp.concatenate([above[rows - near:], tgt, below[rows - near:]], axis=0)
    own = (0, cols_at * 128, 128)[sides]

    def background(field, reach):
        row = lax.broadcasted_iota(jnp.int32, field.shape, 0)
        lane = lax.broadcasted_iota(jnp.int32, field.shape, 1)
        inside = (row >= jnp.where(rows_at == 0, reach, 0)) & (
            row < jnp.where(rows_at == row_end, reach + rows, 2 * reach + rows)
        )
        if sides:
            inside &= (lane >= own - jnp.where(cols_at == 0, 0, reach)) & (
                lane < own + 128 + jnp.where(cols_at == col_end, 0, reach)
            )
        return jnp.where(inside, field + BACKGROUND, 0.0)

    source, target = background(source, far), background(target, near)
    krow = 1.0 - (rows_at == 0).astype(F32) * krow_ref[0] - (rows_at == row_end).astype(F32) * krow_ref[1]
    if sides == 2:
        col_first, col_last = (cols_at == 0).astype(F32), (cols_at == col_end).astype(F32)
        kcol = 1.0 - col_first * kcol_ref[0:1, :] - col_last * kcol_ref[1:2, :]
    else:
        kcol = 1.0 - kcol_ref[0:1, :] - kcol_ref[1:2, :]
    krow = jnp.concatenate([krow] * (1 + sides), axis=1)
    brow = (brow_ref[0], brow_ref[1])
    bcol = (bcol_ref[0], bcol_ref[1])
    if sides == 1:
        last_bcol = tuple(jnp.where(cols_at == 0, band[:, 0:128], band[:, 128:256]) for band in bcol)
    else:
        last_bcol = tuple(band[:, own:own + 128] for band in bcol)

    def smooth(field, count, columns):
        bands = tuple(band[0:count, 0:count + near] for band in brow)
        return product(parts(product(bands, parts(field))), columns)

    def ratio(top, bottom):
        inside = top > 0.0
        return jnp.where(inside, top / jnp.where(inside, bottom, 1.0), 0.0)

    scaling = source / (krow * kcol)
    scaling = ratio(target, smooth(scaling, rows + 2 * near, bcol))
    scaling = ratio(source[near:near + rows + near], smooth(scaling, rows + near, bcol))
    bottom = smooth(scaling, rows, last_bcol)
    middle = scaling[RADIUS:RADIUS + rows]
    if sides == 1:
        source_out[...] = jnp.where(cols_at == 0, middle[:, 0:128], middle[:, 128:256])
    else:
        source_out[...] = middle[:, own:own + 128]
    target_out[...] = (tgt_ref[...] + BACKGROUND) / bottom


def split_table(table):
    high = table.astype(ml_dtypes.bfloat16)
    low = (table - high.astype(np.float64)).astype(ml_dtypes.bfloat16)
    return np.stack([high, low])


def taps():
    offsets = np.arange(-RADIUS, RADIUS + 1, dtype=np.float64)
    weights = np.exp(-4.5 * offsets * offsets / (RADIUS * RADIUS))
    return weights / weights.sum()


def tails(start, count, end):
    weights = taps()
    before, after = np.zeros(count), np.zeros(count)
    for at in range(count):
        if at >= start:
            before[at] = weights[: max(0, RADIUS - (at - start))].sum()
        if at < end:
            after[at] = weights[: max(0, RADIUS - (end - 1 - at))].sum()
    return np.stack([before, after])


def sinkhorn(src, tgt, pair, following, strips):
    rows, cols = src.shape
    sides = len(strips)
    wide = cols * (1 + sides)
    weights = taps()

    def toeplitz(count_out, count_in, shift):
        offset = np.arange(count_in)[None, :] - np.arange(count_out)[:, None] + shift
        inside = (offset >= 0) & (offset <= 2 * RADIUS)
        return np.where(inside, weights[np.clip(offset, 0, 2 * RADIUS)], 0.0)

    brow = split_table(toeplitz(rows + 4 * RADIUS, rows + 6 * RADIUS, 0))
    bcol = split_table(toeplitz(wide, wide, RADIUS))
    krow = tails(3 * RADIUS, rows + 6 * RADIUS, 3 * RADIUS + rows)
    krow = np.broadcast_to(krow[:, :, None], krow.shape + (128,)).astype(np.float32)
    kcol = tails(cols, wide, 2 * cols) if sides == 2 else tails(0, wide, wide)
    kcol = np.concatenate([kcol, np.zeros((6, wide))]).astype(np.float32)
    tables = [jnp.asarray(table) for table in (brow, bcol, krow, kcol)]
    return pl.pallas_call(
        sinkhorn_kernel,
        out_shape=[vmem(rows, cols)] * 2,
        compiler_params=PARAMS,
        cost_estimate=pl.CostEstimate(flops=2000000000, bytes_accessed=1000000, transcendentals=0),
        name="sinkhorn",
    )(*here(src, tgt, pair, following), *here(*tables), *here(*strips))


def finish_kernel(cells, hid, feat, mine_ref, other_ref, source_ref, target_ref, *outs):
    first_out, second_out, output_out, source_out, target_out = outs
    me = lax.axis_index("maps")
    mine, other = mine_ref[...], other_ref[...]
    upper, lower = jnp.where(me == 0, mine, other), jnp.where(me == 0, other, mine)
    cut = hid // 2
    tail = upper[cut:cut + 8]
    inverse = 1.0 / tail[1:2]
    second_out[0:cut, :] = upper[0:cut] * inverse
    second_out[cut:hid, :] = lower[0:cut] * inverse
    first_out[...] = lower[cut:cut + feat] * inverse
    output_out[...] = tail[0:1] * inverse
    source_mean = jnp.where(me == 0, tail[2:3], tail[3:4]) * (1.0 / cells) + BACKGROUND
    target_mean = jnp.where(me == 0, tail[4:5], tail[5:6]) * (1.0 / cells) + BACKGROUND
    ratio = source_mean / target_mean
    source_out[0] = source_ref[...] * (1.0 / (source_mean * ratio))
    target_out[0] = target_ref[...] * (ratio * ratio)


def finish(mine, other, source, target, cells, hid, feat):
    shape = jax.ShapeDtypeStruct((1,) + source.shape, F32)
    return pl.pallas_call(
        functools.partial(finish_kernel, cells, hid, feat),
        out_shape=(
            jax.ShapeDtypeStruct((feat, hid), F32),
            jax.ShapeDtypeStruct((hid, hid), F32),
            jax.ShapeDtypeStruct((1, hid), F32),
            shape,
            shape,
        ),
        compiler_params=PARAMS,
        name="finish",
    )(*here(mine, other, source, target))


def swap(value, axis, step):
    return lax.ppermute(value, axis, [(i, i ^ step) for i in range(lax.axis_size(axis))])


def shift(value, axis, step):
    count = lax.axis_size(axis)
    pairs = [(i, i + step) for i in range(count) if 0 <= i + step < count]
    return lax.ppermute(value, axis, pairs)


def exchange(value, axis, start):
    count = lax.axis_size(axis)
    pairs = [pair for i in range(start, count - 1, 2) for pair in ((i, i + 1), (i + 1, i))]
    return lax.ppermute(value, axis, pairs)


def powers(axis):
    return [1 << k for k in range((lax.axis_size(axis) - 1).bit_length())]


def local(
    drivers, observed, confidence, land_mask, ownership, first_layer, second_layer, output_layer
):
    feat, hid = first_layer.shape
    row_count, col_count = lax.axis_size("rows"), lax.axis_size("cols")
    cells = land_mask.size * row_count * col_count
    sides = min(col_count - 1, 2)
    keep, send, src, tgt, *strips = net(
        drivers, observed, confidence, land_mask, first_layer, second_layer, output_layer, sides
    )
    total = keep + swap(send, "maps", 1)
    if sides == 1:
        strips = [swap(strips[0], "cols", 1)]
    elif sides == 2:
        strips = [shift(strips[0], "cols", 1), shift(strips[1], "cols", -1)]
    for step in powers("cols"):
        total = total + swap(total, "cols", step)
    total, src, tgt, *strips = lax.optimization_barrier((total, src, tgt, *strips))
    to_pair, to_next = halo(src, tgt, strips)
    pair = exchange(to_pair, "rows", 0)
    for at, step in enumerate(powers("rows")):
        total = total + swap(total, "rows", 2 * step - 1)
        if at == 0:
            total, pair, to_next = lax.optimization_barrier((total, pair, to_next))
    following = exchange(to_next, "rows", 1)
    source, target = sinkhorn(src, tgt, pair, following, strips)
    other = swap(total, "maps", 1)
    first, second, output, source, target = finish(total, other, source, target, cells, hid, feat)
    return first, second, output.reshape(hid), source, target


def solution(mesh):
    in_specs = (
        P(("groups", "maps"), None, "rows", "cols"),
        P(("groups", "maps"), "rows", "cols"),
        P(("groups", "maps"), "rows", "cols"),
        P(("groups", "rows"), "cols"),
        P(("groups", "rows"), "cols"),
        P(),
        P(),
        P(),
    )
    out_specs = (
        P("groups", None),
        P("groups", None),
        P("groups"),
        P(("groups", "maps"), "rows", "cols"),
        P(("groups", "maps"), "rows", "cols"),
    )
    return jax.shard_map(local, mesh=mesh, in_specs=in_specs, out_specs=out_specs, check_vma=False)
```

```python
import functools

import jax
import jax.numpy as jnp
import ml_dtypes
import numpy as np
from jax import lax
from jax.experimental import pallas as pl
from jax.experimental.pallas import tpu as pltpu
from jax.sharding import PartitionSpec as P

RADIUS = 24
BACKGROUND = 0.1
UNIT = 8
F32 = jnp.float32
BF = jnp.bfloat16
NT = (((1,), (1,)), ((), ()))


def net_kernel(sides, *refs):
    inputs, refs = refs[0:7], refs[7:]
    keep_out, send_out, src_out, tgt_out = refs[0:4]
    strip_outs, scr = refs[4:4 + sides], refs[4 + sides:]
    held, arrived, scr = scr[-8:-1], scr[-1], scr[:-8]
    copies = [pltpu.make_async_copy(a, b, arrived.at[k]) for k, (a, b) in enumerate(zip(inputs, held))]
    for copy in copies:
        copy.start()
    drv, obs, conf, mask, w1, w2, wo = held
    for copy in copies:
        copy.wait()
    rows = mask.shape[0]
    hid = w2.shape[0]
    feat = w1.shape[0]
    units = rows // UNIT
    wide = UNIT * 128
    TILE = 256
    h1s, s1s, p2s, d2s = scr[0:3], scr[3:6], scr[6:9], scr[9:12]
    xs, obf, wmf, mkf, acc_second, acc_first, acc_outg, wide_wo = scr[12:]
    w1h = (w1[...].astype(F32) * 0.5).T.astype(BF)
    w2f = w2[...].astype(F32)
    w2h = (w2f * 0.5).T.astype(BF)
    w2b = (w2f * 0.5).astype(BF)
    wo_row = wo[...].astype(F32)
    wo_col = jnp.broadcast_to(wo_row, (128, hid)).T
    wide_wo[0] = wo_col
    wide_wo[1] = 0.5 * wo_col
    sub = lax.broadcasted_iota(jnp.int32, (8, 128), 0)
    acc_second[...] = jnp.zeros_like(acc_second)
    acc_first[...] = jnp.zeros_like(acc_first)
    acc_outg[...] = jnp.zeros_like(acc_outg)

    def prepare(i, c):
        r0 = pl.multiple_of(i * 16, 16)
        x3 = jnp.swapaxes(drv[0, :, pl.ds(r0, 16), :].astype(F32), 0, 1).astype(BF)
        xs[:, pl.ds(pl.multiple_of(i * 2048, 2048), 2048)] = jnp.concatenate([x3[r] for r in range(16)], axis=1)
        return c
    lax.fori_loop(0, rows // 16, prepare, 0)
    ob = obs[0].astype(F32)
    mk = mask[...].astype(F32)
    wm = (conf[0].astype(F32) * mk).astype(BF).astype(F32)
    tg = ob * mk
    tgt_out[...] = tg
    obf[...] = ob
    wmf[...] = wm
    mkf[...] = mk

    def one(i, k, f1=True, f2=True, f3=True):
        a, b, c = k % 3, (k + 2) % 3, (k + 1) % 3
        n = wide // TILE
        if f3:
            x_old = xs[:, pl.ds(pl.multiple_of((i - 2) * wide, wide), wide)]
            d2 = d2s[c][...]
        if f1:
            x_new = xs[:, pl.ds(pl.multiple_of(jnp.minimum(i, units - 1) * wide, wide), wide)]
        def s3(j):
            sl = slice(j * TILE, (j + 1) * TILE)
            back = jnp.dot(w2b, d2[:, sl], preferred_element_type=F32)
            d1 = (back * s1s[c][:, sl]).astype(BF)
            acc_first[...] += lax.dot_general(d1, x_old[:, sl], NT, preferred_element_type=F32)
        def s1(j):
            sl = slice(j * TILE, (j + 1) * TILE)
            p1 = jnp.dot(w1h, x_new[:, sl], preferred_element_type=F32)
            t1 = jnp.tanh(p1)
            u1 = 1.0 + t1
            h1 = (p1 * u1).astype(BF)
            h1s[a][:, sl] = h1
            s1s[a][:, sl] = u1 * (1.0 + p1 * (1.0 - t1))
            p2s[a][:, sl] = jnp.dot(w2h, h1, preferred_element_type=F32)
        keep = []
        def s2(r):
            p2 = p2s[b][:, r * 128:(r + 1) * 128]
            t2 = jnp.tanh(p2)
            u2 = 1.0 + t2
            h2 = (p2 * u2).astype(BF)
            s2 = u2 * (1.0 + p2 * (1.0 - t2)) * wide_wo[1]
            keep.append((h2, s2))
        for r in range(8):
            if f2: s2(r)
            if r % (8 // n) == 0:
                if f1: s1(r // (8 // n))
                if f3: s3(r // (8 // n))
        if f3:
            acc_second[...] += lax.dot_general(h1s[c][...], d2, NT, preferred_element_type=F32)
        if not f2: return
        r0 = pl.multiple_of((i - 1) * UNIT, UNIT)
        h2w = jnp.concatenate([h for h, _ in keep], axis=1)
        scs = []
        for h2, _ in keep:
            sc = jnp.sum((h2.astype(F32) * wide_wo[0]).reshape(hid // 8, 8, 128), axis=0)
            for q in (4, 2, 1):
                sc = sc + pltpu.roll(sc, q, 0)
            scs.append(sc)
        score = scs[0]
        for r in range(1, 8):
            score = jnp.where(sub == r, scs[r], score)
        e = jnp.exp(-jnp.abs(score))
        imitated = jnp.maximum(score, 0.0) + jnp.log1p(e)
        sig = jnp.where(score >= 0, 1.0, e) / (1.0 + e)
        delta = wmf[pl.ds(r0, 8), :] * (imitated - obf[pl.ds(r0, 8), :]) * sig
        src_out[pl.ds(r0, 8), :] = mkf[pl.ds(r0, 8), :] * imitated
        mix = []
        high = delta.astype(BF).astype(F32)
        low = delta - high
        for r in range(8):
            h2, s2v = keep[r]
            d8 = jnp.broadcast_to(delta[r:r + 1], (8, 128))
            d = jnp.broadcast_to(d8[None], (hid // 8, 8, 128)).reshape(hid, 128)
            d2s[b][:, r * 128:(r + 1) * 128] = (d * s2v).astype(BF)
            mix.append(jnp.where(sub == 0, high[r:r + 1], jnp.where(sub == 1, low[r:r + 1], 0.0)))
        acc_outg[:, 0:8] += lax.dot_general(
            h2w, jnp.concatenate(mix, axis=1).astype(BF), NT, preferred_element_type=F32
        )

    one(0, 0, True, False, False)
    one(1, 1, True, True, False)
    def body(t, c):
        for k in range(3):
            one(t * 3 + 2 + k, 2 + k)
        return c
    loops = (units - 1 + 2) // 3
    lax.fori_loop(0, loops, body, 0)
    assert loops * 3 + 1 == units
    one(units + 1, units + 1, False, False, True)

    src = src_out[...]
    og = jnp.sum(acc_outg[...].T, axis=0, keepdims=True)
    me = lax.axis_index("maps")
    tot = lambda v: jnp.sum(jnp.sum(v, axis=1, keepdims=True), axis=0, keepdims=True)
    extra = jnp.where(sub == 0, og, 0.0)
    extra = jnp.where(sub == 1, tot(wmf[...]), extra)
    extra = jnp.where(sub == 2 + me, tot(src), extra)
    extra = jnp.where(sub == 4 + me, tot(tgt_out[...]), extra)
    second = acc_second[...]
    cut = hid // 2
    upper = jnp.concatenate([second[0:cut], extra, jnp.zeros((feat - 8, 128), F32)], axis=0)
    lower = jnp.concatenate([second[cut:hid], acc_first[...].T], axis=0)
    keep_out[...] = jnp.where(me == 0, upper, lower)
    send_out[...] = jnp.where(me == 0, lower, upper)
    if sides:
        lanes = lax.broadcasted_iota(jnp.int32, (rows, 128), 1)
        left, right = edge_strips(src, tgt_out[...], lanes)
        strips = [right, left]
        if sides == 1:
            strips = [jnp.where(lax.axis_index("cols") == 0, right, left)]
        for ref, strip in zip(strip_outs, strips):
            ref[...] = strip


def vmem(*shape, dtype=F32):
    return pltpu.VMEM(shape, dtype)


def here(*values):
    return [pltpu.with_memory_space_constraint(value, pltpu.VMEM) for value in values]


PARAMS = pltpu.CompilerParams(vmem_limit_bytes=24 << 20)


def net(drivers, observed, confidence, land_mask, w1, w2, wo, sides):
    feat, hid = w1.shape
    rows, cols = land_mask.shape
    wide = UNIT * cols
    given = (drivers, observed, confidence, land_mask, w1, w2, wo.reshape(1, hid))
    return pl.pallas_call(
        functools.partial(net_kernel, sides),
        out_shape=[vmem(hid // 2 + feat, 128)] * 2
        + [vmem(rows, cols)] * 2
        + [vmem(rows, cols)] * sides,
        scratch_shapes=[vmem(hid, wide, dtype=BF)] * 3
        + [vmem(hid, wide)] * 6
        + [vmem(hid, wide, dtype=BF)] * 3
        + [vmem(feat, rows * cols, dtype=BF)]
        + [vmem(rows, cols)] * 3
        + [vmem(hid, hid), vmem(hid, feat), vmem(hid, 128), vmem(2, hid, 128)]
        + [vmem(*value.shape, dtype=value.dtype) for value in given]
        + [pltpu.SemaphoreType.DMA((len(given),))],
        in_specs=[pl.BlockSpec(memory_space=pl.ANY)] * len(given),
        compiler_params=PARAMS,
        name="net",
    )(*[pltpu.with_memory_space_constraint(value, pltpu.HBM) for value in given])


def edge_strips(src, tgt, lane):
    right = jnp.where(lane >= 128 - 3 * RADIUS, src, pltpu.roll(tgt, 2 * RADIUS, 1))
    left = jnp.where(lane < 3 * RADIUS, src, pltpu.roll(tgt, 128 - 2 * RADIUS, 1))
    return left, right


def widen(src, tgt, strips):
    if not strips:
        return src, tgt
    lane = lax.broadcasted_iota(jnp.int32, src.shape, 1)
    first, last = strips[0][...].astype(F32), strips[-1][...].astype(F32)
    ls = jnp.where(lane >= 128 - 3 * RADIUS, first, 0.0)
    lt = jnp.where(lane >= 128 - 2 * RADIUS, pltpu.roll(first, 128 - 2 * RADIUS, 1), 0.0)
    rs = jnp.where(lane < 3 * RADIUS, last, 0.0)
    rt = jnp.where(lane < 2 * RADIUS, pltpu.roll(last, 2 * RADIUS, 1), 0.0)
    if len(strips) == 2:
        return jnp.concatenate([ls, src, rs], axis=1), jnp.concatenate([lt, tgt, rt], axis=1)
    at_left = lax.axis_index("cols") == 0
    return (
        jnp.concatenate([jnp.where(at_left, src, ls), jnp.where(at_left, rs, src)], axis=1),
        jnp.concatenate([jnp.where(at_left, tgt, lt), jnp.where(at_left, rt, tgt)], axis=1),
    )


def halo_kernel(src_ref, tgt_ref, *refs):
    strips, (near_ref, far_ref) = refs[:-2], refs[-2:]
    src, tgt = widen(src_ref[...], tgt_ref[...], strips)
    rows = src.shape[0]
    far, near = rows - 2 * RADIUS, 2 * RADIUS
    up = jnp.concatenate([src[0:far], tgt[0:near]], axis=0)
    down = jnp.concatenate([src[rows - far:], tgt[rows - near:]], axis=0)
    even = lax.axis_index("rows") % 2 == 0
    near_ref[...] = jnp.where(even, down, up).astype(BF)
    far_ref[...] = jnp.where(even, up, down).astype(BF)


def halo(src, tgt, strips):
    rows, cols = src.shape
    return pl.pallas_call(
        halo_kernel,
        out_shape=[vmem(rows, cols * (1 + len(strips)), dtype=BF)] * 2,
        compiler_params=PARAMS,
        name="halo",
    )(*here(src, tgt, *strips))


def parts(value):
    high = value.astype(BF)
    return high, (value - high.astype(F32)).astype(BF)


def product(left, right):
    (lh, ll), (rh, rl) = left, right
    dot = functools.partial(jnp.dot, preferred_element_type=F32)
    return dot(lh, rh) + (dot(lh, rl) + dot(ll, rh))


def sinkhorn_kernel(src_ref, tgt_ref, pair_ref, next_ref, brow_ref, bcol_ref, krow_ref, kcol_ref, *refs):
    strips = refs[:-2]
    source_out, target_out = refs[-2:]
    sides = len(strips)
    far, near = 3 * RADIUS, 2 * RADIUS
    rows, wide = pair_ref.shape
    rows_at, cols_at = lax.axis_index("rows"), lax.axis_index("cols")
    row_end, col_end = lax.axis_size("rows") - 1, lax.axis_size("cols") - 1
    src, tgt = widen(src_ref[...], tgt_ref[...], strips)
    pair, following = pair_ref[...].astype(F32), next_ref[...].astype(F32)
    even = rows_at % 2 == 0
    above, below = jnp.where(even, following, pair), jnp.where(even, pair, following)
    source = jnp.concatenate([above[rows - near - far:rows - near], src, below[0:far]], axis=0)
    target = jnp.concatenate([above[rows - near:], tgt, below[rows - near:]], axis=0)
    own = (0, cols_at * 128, 128)[sides]

    def background(field, reach):
        row = lax.broadcasted_iota(jnp.int32, field.shape, 0)
        lane = lax.broadcasted_iota(jnp.int32, field.shape, 1)
        inside = (row >= jnp.where(rows_at == 0, reach, 0)) & (
            row < jnp.where(rows_at == row_end, reach + rows, 2 * reach + rows)
        )
        if sides:
            inside &= (lane >= own - jnp.where(cols_at == 0, 0, reach)) & (
                lane < own + 128 + jnp.where(cols_at == col_end, 0, reach)
            )
        return jnp.where(inside, field + BACKGROUND, 0.0)

    source, target = background(source, far), background(target, near)
    krow = 1.0 - (rows_at == 0).astype(F32) * krow_ref[0] - (rows_at == row_end).astype(F32) * krow_ref[1]
    if sides == 2:
        col_first, col_last = (cols_at == 0).astype(F32), (cols_at == col_end).astype(F32)
        kcol = 1.0 - col_first * kcol_ref[0:1, :] - col_last * kcol_ref[1:2, :]
    else:
        kcol = 1.0 - kcol_ref[0:1, :] - kcol_ref[1:2, :]
    krow = jnp.concatenate([krow] * (1 + sides), axis=1)
    brow = (brow_ref[0], brow_ref[1])
    bcol = (bcol_ref[0], bcol_ref[1])
    if sides == 1:
        last_bcol = tuple(jnp.where(cols_at == 0, band[:, 0:128], band[:, 128:256]) for band in bcol)
    else:
        last_bcol = tuple(band[:, own:own + 128] for band in bcol)

    def smooth(field, count, columns):
        bands = tuple(band[0:count, 0:count + near] for band in brow)
        return product(parts(product(bands, parts(field))), columns)

    def ratio(top, bottom):
        inside = top > 0.0
        return jnp.where(inside, top / jnp.where(inside, bottom, 1.0), 0.0)

    scaling = source / (krow * kcol)
    scaling = ratio(target, smooth(scaling, rows + 2 * near, bcol))
    scaling = ratio(source[near:near + rows + near], smooth(scaling, rows + near, bcol))
    bottom = smooth(scaling, rows, last_bcol)
    middle = scaling[RADIUS:RADIUS + rows]
    if sides == 1:
        source_out[...] = jnp.where(cols_at == 0, middle[:, 0:128], middle[:, 128:256])
    else:
        source_out[...] = middle[:, own:own + 128]
    target_out[...] = (tgt_ref[...] + BACKGROUND) / bottom


def split_table(table):
    high = table.astype(ml_dtypes.bfloat16)
    low = (table - high.astype(np.float64)).astype(ml_dtypes.bfloat16)
    return np.stack([high, low])


def taps():
    offsets = np.arange(-RADIUS, RADIUS + 1, dtype=np.float64)
    weights = np.exp(-4.5 * offsets * offsets / (RADIUS * RADIUS))
    return weights / weights.sum()


def tails(start, count, end):
    weights = taps()
    before, after = np.zeros(count), np.zeros(count)
    for at in range(count):
        if at >= start:
            before[at] = weights[: max(0, RADIUS - (at - start))].sum()
        if at < end:
            after[at] = weights[: max(0, RADIUS - (end - 1 - at))].sum()
    return np.stack([before, after])


def sinkhorn(src, tgt, pair, following, strips):
    rows, cols = src.shape
    sides = len(strips)
    wide = cols * (1 + sides)
    weights = taps()

    def toeplitz(count_out, count_in, shift):
        offset = np.arange(count_in)[None, :] - np.arange(count_out)[:, None] + shift
        inside = (offset >= 0) & (offset <= 2 * RADIUS)
        return np.where(inside, weights[np.clip(offset, 0, 2 * RADIUS)], 0.0)

    brow = split_table(toeplitz(rows + 4 * RADIUS, rows + 6 * RADIUS, 0))
    bcol = split_table(toeplitz(wide, wide, RADIUS))
    krow = tails(3 * RADIUS, rows + 6 * RADIUS, 3 * RADIUS + rows)
    krow = np.broadcast_to(krow[:, :, None], krow.shape + (128,)).astype(np.float32)
    kcol = tails(cols, wide, 2 * cols) if sides == 2 else tails(0, wide, wide)
    kcol = np.concatenate([kcol, np.zeros((6, wide))]).astype(np.float32)
    tables = [jnp.asarray(table) for table in (brow, bcol, krow, kcol)]
    return pl.pallas_call(
        sinkhorn_kernel,
        out_shape=[vmem(rows, cols)] * 2,
        compiler_params=PARAMS,
        cost_estimate=pl.CostEstimate(flops=2000000000, bytes_accessed=1000000, transcendentals=0),
        name="sinkhorn",
    )(*here(src, tgt, pair, following), *here(*tables), *here(*strips))


def finish_kernel(cells, hid, feat, mine_ref, other_ref, source_ref, target_ref, *outs):
    first_out, second_out, output_out, source_out, target_out = outs
    me = lax.axis_index("maps")
    mine, other = mine_ref[...], other_ref[...]
    upper, lower = jnp.where(me == 0, mine, other), jnp.where(me == 0, other, mine)
    cut = hid // 2
    tail = upper[cut:cut + 8]
    inverse = 1.0 / tail[1:2]
    second_out[0:cut, :] = upper[0:cut] * inverse
    second_out[cut:hid, :] = lower[0:cut] * inverse
    first_out[...] = lower[cut:cut + feat] * inverse
    output_out[...] = tail[0:1] * inverse
    source_mean = jnp.where(me == 0, tail[2:3], tail[3:4]) * (1.0 / cells) + BACKGROUND
    target_mean = jnp.where(me == 0, tail[4:5], tail[5:6]) * (1.0 / cells) + BACKGROUND
    ratio = source_mean / target_mean
    source_out[0] = source_ref[...] * (1.0 / (source_mean * ratio))
    target_out[0] = target_ref[...] * (ratio * ratio)


def finish(mine, other, source, target, cells, hid, feat):
    shape = jax.ShapeDtypeStruct((1,) + source.shape, F32)
    return pl.pallas_call(
        functools.partial(finish_kernel, cells, hid, feat),
        out_shape=(
            jax.ShapeDtypeStruct((feat, hid), F32),
            jax.ShapeDtypeStruct((hid, hid), F32),
            jax.ShapeDtypeStruct((1, hid), F32),
            shape,
            shape,
        ),
        compiler_params=PARAMS,
        name="finish",
    )(*here(mine, other, source, target))


def swap(value, axis, step):
    return lax.ppermute(value, axis, [(i, i ^ step) for i in range(lax.axis_size(axis))])


def shift(value, axis, step):
    count = lax.axis_size(axis)
    pairs = [(i, i + step) for i in range(count) if 0 <= i + step < count]
    return lax.ppermute(value, axis, pairs)


def exchange(value, axis, start):
    count = lax.axis_size(axis)
    pairs = [pair for i in range(start, count - 1, 2) for pair in ((i, i + 1), (i + 1, i))]
    return lax.ppermute(value, axis, pairs)


def powers(axis):
    return [1 << k for k in range((lax.axis_size(axis) - 1).bit_length())]


def local(
    drivers, observed, confidence, land_mask, ownership, first_layer, second_layer, output_layer
):
    feat, hid = first_layer.shape
    row_count, col_count = lax.axis_size("rows"), lax.axis_size("cols")
    cells = land_mask.size * row_count * col_count
    sides = min(col_count - 1, 2)
    keep, send, src, tgt, *strips = net(
        drivers, observed, confidence, land_mask, first_layer, second_layer, output_layer, sides
    )
    total = keep + swap(send, "maps", 1)
    if sides == 1:
        strips = [swap(strips[0], "cols", 1)]
    elif sides == 2:
        strips = [shift(strips[0], "cols", 1), shift(strips[1], "cols", -1)]
    for step in powers("cols"):
        total = total + swap(total, "cols", step)
    to_pair, to_next = halo(src, tgt, strips)
    pair = exchange(to_pair, "rows", 0)
    for at, step in enumerate(powers("rows")):
        total = total + swap(total, "rows", 2 * step - 1)
        if at == 0:
            total, pair, to_next = lax.optimization_barrier((total, pair, to_next))
    following = exchange(to_next, "rows", 1)
    source, target = sinkhorn(src, tgt, pair, following, strips)
    other = swap(total, "maps", 1)
    first, second, output, source, target = finish(total, other, source, target, cells, hid, feat)
    return first, second, output.reshape(hid), source, target


def solution(mesh):
    in_specs = (
        P(("groups", "maps"), None, "rows", "cols"),
        P(("groups", "maps"), "rows", "cols"),
        P(("groups", "maps"), "rows", "cols"),
        P(("groups", "rows"), "cols"),
        P(("groups", "rows"), "cols"),
        P(),
        P(),
        P(),
    )
    out_specs = (
        P("groups", None),
        P("groups", None),
        P("groups"),
        P(("groups", "maps"), "rows", "cols"),
        P(("groups", "maps"), "rows", "cols"),
    )
    return jax.shard_map(local, mesh=mesh, in_specs=in_specs, out_specs=out_specs, check_vma=False)
```

```python
import functools

import jax
import jax.numpy as jnp
import ml_dtypes
import numpy as np
from jax import lax
from jax.experimental import pallas as pl
from jax.experimental.pallas import tpu as pltpu
from jax.sharding import PartitionSpec as P

RADIUS = 24
BACKGROUND = 0.1
UNIT = 8
F32 = jnp.float32
BF = jnp.bfloat16
NT = (((1,), (1,)), ((), ()))


def net_kernel(sides, *refs):
    inputs, refs = refs[0:7], refs[7:]
    keep_out, send_out, src_out, tgt_out = refs[0:4]
    strip_outs, scr = refs[4:4 + sides], refs[4 + sides:]
    held, arrived, scr = scr[-8:-1], scr[-1], scr[:-8]
    copies = [pltpu.make_async_copy(a, b, arrived.at[k]) for k, (a, b) in enumerate(zip(inputs, held))]
    for copy in copies:
        copy.start()
    drv, obs, conf, mask, w1, w2, wo = held
    for copy in copies:
        copy.wait()
    rows = mask.shape[0]
    hid = w2.shape[0]
    feat = w1.shape[0]
    units = rows // UNIT
    wide = UNIT * 128
    TILE = 256
    h1s, s1s, p2s, d2s = scr[0:3], scr[3:6], scr[6:9], scr[9:12]
    xs, obf, wmf, mkf, acc_second, acc_first, acc_outg, wide_wo = scr[12:]
    w1h = (w1[...].astype(F32) * 0.5).T.astype(BF)
    w2f = w2[...].astype(F32)
    w2h = (w2f * 0.5).T.astype(BF)
    w2b = (w2f * 0.5).astype(BF)
    wo_row = wo[...].astype(F32)
    wo_col = jnp.broadcast_to(wo_row, (128, hid)).T
    wide_wo[0] = wo_col
    wide_wo[1] = 0.5 * wo_col
    sub = lax.broadcasted_iota(jnp.int32, (8, 128), 0)
    acc_second[...] = jnp.zeros_like(acc_second)
    acc_first[...] = jnp.zeros_like(acc_first)
    acc_outg[...] = jnp.zeros_like(acc_outg)

    def prepare(i, c):
        r0 = pl.multiple_of(i * 16, 16)
        x3 = jnp.swapaxes(drv[0, :, pl.ds(r0, 16), :].astype(F32), 0, 1).astype(BF)
        xs[:, pl.ds(pl.multiple_of(i * 2048, 2048), 2048)] = jnp.concatenate([x3[r] for r in range(16)], axis=1)
        return c
    lax.fori_loop(0, rows // 16, prepare, 0)
    ob = obs[0].astype(F32)
    mk = mask[...].astype(F32)
    wm = (conf[0].astype(F32) * mk).astype(BF).astype(F32)
    tg = ob * mk
    tgt_out[...] = tg
    obf[...] = ob
    wmf[...] = wm
    mkf[...] = mk
    tot = lambda v: jnp.sum(jnp.sum(v, axis=1, keepdims=True), axis=0, keepdims=True)
    weight_sum, target_sum = tot(wm), tot(tg)

    def one(i, k, f1=True, f2=True, f3=True):
        a, b, c = k % 3, (k + 2) % 3, (k + 1) % 3
        n = wide // TILE
        if f3:
            x_old = xs[:, pl.ds(pl.multiple_of((i - 2) * wide, wide), wide)]
            d2 = d2s[c][...]
        if f1:
            x_new = xs[:, pl.ds(pl.multiple_of(jnp.minimum(i, units - 1) * wide, wide), wide)]
        def s3(j):
            sl = slice(j * TILE, (j + 1) * TILE)
            back = jnp.dot(w2b, d2[:, sl], preferred_element_type=F32)
            d1 = (back * s1s[c][:, sl]).astype(BF)
            acc_first[...] += lax.dot_general(d1, x_old[:, sl], NT, preferred_element_type=F32)
        def s1(j):
            sl = slice(j * TILE, (j + 1) * TILE)
            p1 = jnp.dot(w1h, x_new[:, sl], preferred_element_type=F32)
            t1 = jnp.tanh(p1)
            u1 = 1.0 + t1
            h1 = (p1 * u1).astype(BF)
            h1s[a][:, sl] = h1
            s1s[a][:, sl] = u1 * (1.0 + p1 * (1.0 - t1))
            p2s[a][:, sl] = jnp.dot(w2h, h1, preferred_element_type=F32)
        keep = []
        def s2(r):
            p2 = p2s[b][:, r * 128:(r + 1) * 128]
            t2 = jnp.tanh(p2)
            u2 = 1.0 + t2
            h2 = (p2 * u2).astype(BF)
            s2 = u2 * (1.0 + p2 * (1.0 - t2)) * wide_wo[1]
            keep.append((h2, s2))
        for r in range(8):
            if f2: s2(r)
            if r % (8 // n) == 0:
                if f1: s1(r // (8 // n))
                if f3: s3(r // (8 // n))
        if f3:
            acc_second[...] += lax.dot_general(h1s[c][...], d2, NT, preferred_element_type=F32)
        if not f2: return
        r0 = pl.multiple_of((i - 1) * UNIT, UNIT)
        h2w = jnp.concatenate([h for h, _ in keep], axis=1)
        scs = []
        for h2, _ in keep:
            sc = jnp.sum((h2.astype(F32) * wide_wo[0]).reshape(hid // 8, 8, 128), axis=0)
            for q in (4, 2, 1):
                sc = sc + pltpu.roll(sc, q, 0)
            scs.append(sc)
        score = scs[0]
        for r in range(1, 8):
            score = jnp.where(sub == r, scs[r], score)
        e = jnp.exp(-jnp.abs(score))
        imitated = jnp.maximum(score, 0.0) + jnp.log1p(e)
        sig = jnp.where(score >= 0, 1.0, e) / (1.0 + e)
        delta = wmf[pl.ds(r0, 8), :] * (imitated - obf[pl.ds(r0, 8), :]) * sig
        src_out[pl.ds(r0, 8), :] = mkf[pl.ds(r0, 8), :] * imitated
        mix = []
        high = delta.astype(BF).astype(F32)
        low = delta - high
        for r in range(8):
            h2, s2v = keep[r]
            d8 = jnp.broadcast_to(delta[r:r + 1], (8, 128))
            d = jnp.broadcast_to(d8[None], (hid // 8, 8, 128)).reshape(hid, 128)
            d2s[b][:, r * 128:(r + 1) * 128] = (d * s2v).astype(BF)
            mix.append(jnp.where(sub == 0, high[r:r + 1], jnp.where(sub == 1, low[r:r + 1], 0.0)))
        acc_outg[:, 0:8] += lax.dot_general(
            h2w, jnp.concatenate(mix, axis=1).astype(BF), NT, preferred_element_type=F32
        )

    one(0, 0, True, False, False)
    one(1, 1, True, True, False)
    def body(t, c):
        for k in range(3):
            one(t * 3 + 2 + k, 2 + k)
        return c
    loops = (units - 1 + 2) // 3
    lax.fori_loop(0, loops, body, 0)
    assert loops * 3 + 1 == units
    one(units + 1, units + 1, False, False, True)

    src = src_out[...]
    og = jnp.sum(acc_outg[...].T, axis=0, keepdims=True)
    me = lax.axis_index("maps")
    extra = jnp.where(sub == 0, og, 0.0)
    extra = jnp.where(sub == 1, weight_sum, extra)
    extra = jnp.where(sub == 2 + me, tot(src), extra)
    extra = jnp.where(sub == 4 + me, target_sum, extra)
    second = acc_second[...]
    cut = hid // 2
    upper = jnp.concatenate([second[0:cut], extra, jnp.zeros((feat - 8, 128), F32)], axis=0)
    lower = jnp.concatenate([second[cut:hid], acc_first[...].T], axis=0)
    keep_out[...] = jnp.where(me == 0, upper, lower)
    send_out[...] = jnp.where(me == 0, lower, upper)
    if sides:
        lanes = lax.broadcasted_iota(jnp.int32, (rows, 128), 1)
        left, right = edge_strips(src, tgt_out[...], lanes)
        strips = [right, left]
        if sides == 1:
            strips = [jnp.where(lax.axis_index("cols") == 0, right, left)]
        for ref, strip in zip(strip_outs, strips):
            ref[...] = strip


def vmem(*shape, dtype=F32):
    return pltpu.VMEM(shape, dtype)


def here(*values):
    return [pltpu.with_memory_space_constraint(value, pltpu.VMEM) for value in values]


PARAMS = pltpu.CompilerParams(vmem_limit_bytes=24 << 20)


def net(drivers, observed, confidence, land_mask, w1, w2, wo, sides):
    feat, hid = w1.shape
    rows, cols = land_mask.shape
    wide = UNIT * cols
    given = (drivers, observed, confidence, land_mask, w1, w2, wo.reshape(1, hid))
    return pl.pallas_call(
        functools.partial(net_kernel, sides),
        out_shape=[vmem(hid // 2 + feat, 128)] * 2
        + [vmem(rows, cols)] * 2
        + [vmem(rows, cols)] * sides,
        scratch_shapes=[vmem(hid, wide, dtype=BF)] * 3
        + [vmem(hid, wide)] * 6
        + [vmem(hid, wide, dtype=BF)] * 3
        + [vmem(feat, rows * cols, dtype=BF)]
        + [vmem(rows, cols)] * 3
        + [vmem(hid, hid), vmem(hid, feat), vmem(hid, 128), vmem(2, hid, 128)]
        + [vmem(*value.shape, dtype=value.dtype) for value in given]
        + [pltpu.SemaphoreType.DMA((len(given),))],
        in_specs=[pl.BlockSpec(memory_space=pl.ANY)] * len(given),
        compiler_params=PARAMS,
        name="net",
    )(*[pltpu.with_memory_space_constraint(value, pltpu.HBM) for value in given])


def edge_strips(src, tgt, lane):
    right = jnp.where(lane >= 128 - 3 * RADIUS, src, pltpu.roll(tgt, 2 * RADIUS, 1))
    left = jnp.where(lane < 3 * RADIUS, src, pltpu.roll(tgt, 128 - 2 * RADIUS, 1))
    return left, right


def widen(src, tgt, strips):
    if not strips:
        return src, tgt
    lane = lax.broadcasted_iota(jnp.int32, src.shape, 1)
    first, last = strips[0][...].astype(F32), strips[-1][...].astype(F32)
    ls = jnp.where(lane >= 128 - 3 * RADIUS, first, 0.0)
    lt = jnp.where(lane >= 128 - 2 * RADIUS, pltpu.roll(first, 128 - 2 * RADIUS, 1), 0.0)
    rs = jnp.where(lane < 3 * RADIUS, last, 0.0)
    rt = jnp.where(lane < 2 * RADIUS, pltpu.roll(last, 2 * RADIUS, 1), 0.0)
    if len(strips) == 2:
        return jnp.concatenate([ls, src, rs], axis=1), jnp.concatenate([lt, tgt, rt], axis=1)
    at_left = lax.axis_index("cols") == 0
    return (
        jnp.concatenate([jnp.where(at_left, src, ls), jnp.where(at_left, rs, src)], axis=1),
        jnp.concatenate([jnp.where(at_left, tgt, lt), jnp.where(at_left, rt, tgt)], axis=1),
    )


def halo_kernel(src_ref, tgt_ref, *refs):
    strips, (near_ref, far_ref) = refs[:-2], refs[-2:]
    src, tgt = widen(src_ref[...], tgt_ref[...], strips)
    rows = src.shape[0]
    far, near = rows - 2 * RADIUS, 2 * RADIUS
    up = jnp.concatenate([src[0:far], tgt[0:near]], axis=0)
    down = jnp.concatenate([src[rows - far:], tgt[rows - near:]], axis=0)
    even = lax.axis_index("rows") % 2 == 0
    near_ref[...] = jnp.where(even, down, up).astype(BF)
    far_ref[...] = jnp.where(even, up, down).astype(BF)


def halo(src, tgt, strips):
    rows, cols = src.shape
    return pl.pallas_call(
        halo_kernel,
        out_shape=[vmem(rows, cols * (1 + len(strips)), dtype=BF)] * 2,
        compiler_params=PARAMS,
        name="halo",
    )(*here(src, tgt, *strips))


def parts(value):
    high = value.astype(BF)
    return high, (value - high.astype(F32)).astype(BF)


def product(left, right):
    (lh, ll), (rh, rl) = left, right
    dot = functools.partial(jnp.dot, preferred_element_type=F32)
    return dot(lh, rh) + (dot(lh, rl) + dot(ll, rh))


def sinkhorn_kernel(src_ref, tgt_ref, pair_ref, next_ref, brow_ref, bcol_ref, krow_ref, kcol_ref, *refs):
    strips = refs[:-2]
    source_out, target_out = refs[-2:]
    sides = len(strips)
    far, near = 3 * RADIUS, 2 * RADIUS
    rows, wide = pair_ref.shape
    rows_at, cols_at = lax.axis_index("rows"), lax.axis_index("cols")
    row_end, col_end = lax.axis_size("rows") - 1, lax.axis_size("cols") - 1
    src, tgt = widen(src_ref[...], tgt_ref[...], strips)
    pair, following = pair_ref[...].astype(F32), next_ref[...].astype(F32)
    even = rows_at % 2 == 0
    above, below = jnp.where(even, following, pair), jnp.where(even, pair, following)
    source = jnp.concatenate([above[rows - near - far:rows - near], src, below[0:far]], axis=0)
    target = jnp.concatenate([above[rows - near:], tgt, below[rows - near:]], axis=0)
    own = (0, cols_at * 128, 128)[sides]

    def background(field, reach):
        row = lax.broadcasted_iota(jnp.int32, field.shape, 0)
        lane = lax.broadcasted_iota(jnp.int32, field.shape, 1)
        inside = (row >= jnp.where(rows_at == 0, reach, 0)) & (
            row < jnp.where(rows_at == row_end, reach + rows, 2 * reach + rows)
        )
        if sides:
            inside &= (lane >= own - jnp.where(cols_at == 0, 0, reach)) & (
                lane < own + 128 + jnp.where(cols_at == col_end, 0, reach)
            )
        return jnp.where(inside, field + BACKGROUND, 0.0)

    source, target = background(source, far), background(target, near)
    krow = 1.0 - (rows_at == 0).astype(F32) * krow_ref[0] - (rows_at == row_end).astype(F32) * krow_ref[1]
    if sides == 2:
        col_first, col_last = (cols_at == 0).astype(F32), (cols_at == col_end).astype(F32)
        kcol = 1.0 - col_first * kcol_ref[0:1, :] - col_last * kcol_ref[1:2, :]
    else:
        kcol = 1.0 - kcol_ref[0:1, :] - kcol_ref[1:2, :]
    krow = jnp.concatenate([krow] * (1 + sides), axis=1)
    brow = (brow_ref[0], brow_ref[1])
    bcol = (bcol_ref[0], bcol_ref[1])
    if sides == 1:
        last_bcol = tuple(jnp.where(cols_at == 0, band[:, 0:128], band[:, 128:256]) for band in bcol)
    else:
        last_bcol = tuple(band[:, own:own + 128] for band in bcol)

    def smooth(field, count, columns):
        bands = tuple(band[0:count, 0:count + near] for band in brow)
        return product(parts(product(bands, parts(field))), columns)

    def ratio(top, bottom):
        inside = top > 0.0
        return jnp.where(inside, top / jnp.where(inside, bottom, 1.0), 0.0)

    scaling = source / (krow * kcol)
    scaling = ratio(target, smooth(scaling, rows + 2 * near, bcol))
    scaling = ratio(source[near:near + rows + near], smooth(scaling, rows + near, bcol))
    bottom = smooth(scaling, rows, last_bcol)
    middle = scaling[RADIUS:RADIUS + rows]
    if sides == 1:
        source_out[...] = jnp.where(cols_at == 0, middle[:, 0:128], middle[:, 128:256])
    else:
        source_out[...] = middle[:, own:own + 128]
    target_out[...] = (tgt_ref[...] + BACKGROUND) / bottom


def split_table(table):
    high = table.astype(ml_dtypes.bfloat16)
    low = (table - high.astype(np.float64)).astype(ml_dtypes.bfloat16)
    return np.stack([high, low])


def taps():
    offsets = np.arange(-RADIUS, RADIUS + 1, dtype=np.float64)
    weights = np.exp(-4.5 * offsets * offsets / (RADIUS * RADIUS))
    return weights / weights.sum()


def tails(start, count, end):
    weights = taps()
    before, after = np.zeros(count), np.zeros(count)
    for at in range(count):
        if at >= start:
            before[at] = weights[: max(0, RADIUS - (at - start))].sum()
        if at < end:
            after[at] = weights[: max(0, RADIUS - (end - 1 - at))].sum()
    return np.stack([before, after])


def sinkhorn(src, tgt, pair, following, strips):
    rows, cols = src.shape
    sides = len(strips)
    wide = cols * (1 + sides)
    weights = taps()

    def toeplitz(count_out, count_in, shift):
        offset = np.arange(count_in)[None, :] - np.arange(count_out)[:, None] + shift
        inside = (offset >= 0) & (offset <= 2 * RADIUS)
        return np.where(inside, weights[np.clip(offset, 0, 2 * RADIUS)], 0.0)

    brow = split_table(toeplitz(rows + 4 * RADIUS, rows + 6 * RADIUS, 0))
    bcol = split_table(toeplitz(wide, wide, RADIUS))
    krow = tails(3 * RADIUS, rows + 6 * RADIUS, 3 * RADIUS + rows)
    krow = np.broadcast_to(krow[:, :, None], krow.shape + (128,)).astype(np.float32)
    kcol = tails(cols, wide, 2 * cols) if sides == 2 else tails(0, wide, wide)
    kcol = np.concatenate([kcol, np.zeros((6, wide))]).astype(np.float32)
    tables = [jnp.asarray(table) for table in (brow, bcol, krow, kcol)]
    return pl.pallas_call(
        sinkhorn_kernel,
        out_shape=[vmem(rows, cols)] * 2,
        compiler_params=PARAMS,
        cost_estimate=pl.CostEstimate(flops=2000000000, bytes_accessed=1000000, transcendentals=0),
        name="sinkhorn",
    )(*here(src, tgt, pair, following), *here(*tables), *here(*strips))


def finish_kernel(cells, hid, feat, mine_ref, other_ref, source_ref, target_ref, *outs):
    first_out, second_out, output_out, source_out, target_out = outs
    me = lax.axis_index("maps")
    mine, other = mine_ref[...], other_ref[...]
    upper, lower = jnp.where(me == 0, mine, other), jnp.where(me == 0, other, mine)
    cut = hid // 2
    tail = upper[cut:cut + 8]
    inverse = 1.0 / tail[1:2]
    second_out[0:cut, :] = upper[0:cut] * inverse
    second_out[cut:hid, :] = lower[0:cut] * inverse
    first_out[...] = lower[cut:cut + feat] * inverse
    output_out[...] = tail[0:1] * inverse
    source_mean = jnp.where(me == 0, tail[2:3], tail[3:4]) * (1.0 / cells) + BACKGROUND
    target_mean = jnp.where(me == 0, tail[4:5], tail[5:6]) * (1.0 / cells) + BACKGROUND
    ratio = source_mean / target_mean
    source_out[0] = source_ref[...] * (1.0 / (source_mean * ratio))
    target_out[0] = target_ref[...] * (ratio * ratio)


def finish(mine, other, source, target, cells, hid, feat):
    shape = jax.ShapeDtypeStruct((1,) + source.shape, F32)
    return pl.pallas_call(
        functools.partial(finish_kernel, cells, hid, feat),
        out_shape=(
            jax.ShapeDtypeStruct((feat, hid), F32),
            jax.ShapeDtypeStruct((hid, hid), F32),
            jax.ShapeDtypeStruct((1, hid), F32),
            shape,
            shape,
        ),
        compiler_params=PARAMS,
        name="finish",
    )(*here(mine, other, source, target))


def swap(value, axis, step):
    return lax.ppermute(value, axis, [(i, i ^ step) for i in range(lax.axis_size(axis))])


def shift(value, axis, step):
    count = lax.axis_size(axis)
    pairs = [(i, i + step) for i in range(count) if 0 <= i + step < count]
    return lax.ppermute(value, axis, pairs)


def exchange(value, axis, start):
    count = lax.axis_size(axis)
    pairs = [pair for i in range(start, count - 1, 2) for pair in ((i, i + 1), (i + 1, i))]
    return lax.ppermute(value, axis, pairs)


def powers(axis):
    return [1 << k for k in range((lax.axis_size(axis) - 1).bit_length())]


def local(
    drivers, observed, confidence, land_mask, ownership, first_layer, second_layer, output_layer
):
    feat, hid = first_layer.shape
    row_count, col_count = lax.axis_size("rows"), lax.axis_size("cols")
    cells = land_mask.size * row_count * col_count
    sides = min(col_count - 1, 2)
    keep, send, src, tgt, *strips = net(
        drivers, observed, confidence, land_mask, first_layer, second_layer, output_layer, sides
    )
    total = keep + swap(send, "maps", 1)
    if sides == 1:
        strips = [swap(strips[0], "cols", 1)]
    elif sides == 2:
        strips = [shift(strips[0], "cols", 1), shift(strips[1], "cols", -1)]
    for step in powers("cols"):
        total = total + swap(total, "cols", step)
    to_pair, to_next = halo(src, tgt, strips)
    pair = exchange(to_pair, "rows", 0)
    for at, step in enumerate(powers("rows")):
        total = total + swap(total, "rows", 2 * step - 1)
        if at == 0:
            total, pair, to_next = lax.optimization_barrier((total, pair, to_next))
    following = exchange(to_next, "rows", 1)
    source, target = sinkhorn(src, tgt, pair, following, strips)
    other = swap(total, "maps", 1)
    first, second, output, source, target = finish(total, other, source, target, cells, hid, feat)
    return first, second, output.reshape(hid), source, target


def solution(mesh):
    in_specs = (
        P(("groups", "maps"), None, "rows", "cols"),
        P(("groups", "maps"), "rows", "cols"),
        P(("groups", "maps"), "rows", "cols"),
        P(("groups", "rows"), "cols"),
        P(("groups", "rows"), "cols"),
        P(),
        P(),
        P(),
    )
    out_specs = (
        P("groups", None),
        P("groups", None),
        P("groups"),
        P(("groups", "maps"), "rows", "cols"),
        P(("groups", "maps"), "rows", "cols"),
    )
    return jax.shard_map(local, mesh=mesh, in_specs=in_specs, out_specs=out_specs, check_vma=False)
```
